32 devices in a mesh: rows: 4 (over y, x), cols: 8 (over z, core).
Axes of the slice: x: 2, y: 2, z: 4, core: 2. Of those that a mesh axis runs over, the one named last changes fastest.
Arguments:
- coefficients: float32 [1024, 2048], P('cols', 'rows'), may hold values from -6 to 6
- factor_panel: float32 [2048, 1024], P('rows'), may hold values from -0.125 to 0.125
- block_inverse: float32 [2048, 512], P('rows'), may hold values from -0.044194174 to 2, as said below
- train_inputs: float32 [14, 2048], P(None, 'rows'), may hold values from 0 to 1
- query_points: float32 [14, 8192], replicated, may hold values from 0 to 1
- inv_length: float32 [14], replicated, may hold values from 0.25 to 2
- amplitude: float32 [1024], P('cols'), may hold values from 0.02 to 0.2
Outputs:
- weights: float32 [1024, 2048], P('cols', 'rows')
- predicted_mean: float32 [1024, 8192], P('cols', 'rows')
The draws below stay inside these ranges and needn't reach their ends.
Inputs may be any that keep to these rules, and one draw needn't show every extreme that they name: `block_inverse`: each block of 512 rows is lower triangular, with diagonal entries from 1 to 2.
All inputs are finite; a program needn't handle non-finite values.
Results may differ from the reference program's by a relative error of at most 0.004.
Values may be sent and summed in bfloat16 or wider, within the bound.
A program may use at most 64 MiB of HBM per device.

```python
import math
import jax
import jax.numpy as jnp
from jax import lax

M = 1024
PARAMS = 14
BLK = 512
QRY = 8192
N_TRAIN = 2048


def draw_block_inverse(key, part):
    first_key, second_key = jax.random.split(key)
    row_ids = (jnp.arange(N_TRAIN) % BLK)[:, None]
    col_ids = jnp.arange(BLK)[None, :]
    below = jax.random.uniform(first_key, (N_TRAIN, BLK), jnp.float32, -1.0, 1.0) * BLK ** (-0.5)
    on_diag = jax.random.uniform(second_key, (N_TRAIN, BLK), jnp.float32, 1.0, 2.0)
    return jnp.where(col_ids == row_ids, on_diag, jnp.where(col_ids < row_ids, below, 0.0))


def block_scale(own_key, extent, shards, smallest, top_value):
    def one(axis_at, blocks):
        draws = jax.random.uniform(jax.random.fold_in(jax.random.fold_in(own_key, 6), axis_at), (blocks,), jnp.float32, smallest / len(shards), top_value / len(shards))
        return jnp.repeat(jnp.exp(draws), extent[axis_at] // blocks).reshape((-1,) + (1,) * (len(extent) - axis_at - 1))

    gain = one(*shards[0])
    for cut in shards[1:]:
        gain = gain * one(*cut)
    return gain


def normal_values(stream_key, shape, deviation, most, shards=(), kind=jnp.bfloat16):
    gain = block_scale(stream_key, shape, shards, -0.22, 0.18) if shards else 1.0
    entries = jax.random.normal(stream_key, shape, jnp.float32) * deviation * gain
    return jnp.minimum(jnp.maximum(entries, -most), most).astype(kind)


def setup_inputs(seed: int = 0) -> dict:
    key_list = jax.random.split(jax.random.key(seed), 8)
    return {
        "coefficients": normal_values(key_list[0], (M, N_TRAIN), 1.0, 6.0, ((0, 8), (1, 4)), jnp.float32),
        "factor_panel": normal_values(key_list[1], (N_TRAIN, 2 * BLK), N_TRAIN ** -0.5, 0.125, ((0, 4),), jnp.float32),
        "block_inverse": draw_block_inverse(jax.random.fold_in(key_list[7], 71), 0),
        "train_inputs": jnp.clip(1.0 * jax.random.uniform(key_list[3], (PARAMS, N_TRAIN), jnp.float32) ** block_scale(key_list[3], (PARAMS, N_TRAIN), ((1, 4),), -0.2, 0.2), 0.0, 1.0),
        "query_points": jnp.clip(jax.random.uniform(key_list[4], (PARAMS, QRY), jnp.float32, 0.0, 1.0), 0.0, 1.0),
        "inv_length": jnp.clip(jnp.exp(jax.random.uniform(key_list[5], (PARAMS,), jnp.float32, math.log(0.25), math.log(2.0))), 0.25, 2.0),
        "amplitude": jnp.clip(jnp.exp(math.log(0.2) - 2.3025851 * jax.random.uniform(key_list[6], (M,), jnp.float32) ** block_scale(key_list[6], (M,), ((0, 8),), -0.2, 0.2)), 0.02, 0.2),
    }


def kernel_values(train_part, query_part, inv_length):
    squared = jnp.zeros((train_part.shape[1], query_part.shape[1]), jnp.float32)
    for dim_index in range(train_part.shape[0]):
        offset = (train_part[dim_index][:, None] - query_part[dim_index][None, :]) * inv_length[dim_index]
        squared = squared + offset * offset
    return jnp.exp(-jnp.sqrt(squared + 1e-06)).astype(jnp.bfloat16)

def solve_product(left, right):
    return jnp.dot(left, right, precision=lax.Precision.HIGHEST, preferred_element_type=jnp.float32)

def reference(coefficients, factor_panel, block_inverse, train_inputs, query_points, inv_length, amplitude):
    block_len = BLK
    solved_rest = coefficients[:, 2 * block_len:]
    rest_one = solve_product(solved_rest, factor_panel[2 * block_len:, block_len:])
    weights_one = solve_product(coefficients[:, block_len:2 * block_len] - rest_one, block_inverse[block_len:2 * block_len])
    rest_zero = solve_product(solved_rest, factor_panel[2 * block_len:, :block_len]) + solve_product(weights_one, factor_panel[block_len:2 * block_len, :block_len])
    weights_zero = solve_product(coefficients[:, :block_len] - rest_zero, block_inverse[:block_len])
    weights = jnp.concatenate([weights_zero, weights_one, solved_rest], axis=1)
    weights_low = weights.astype(jnp.bfloat16)
    span_len = math.gcd(QRY, 512)
    span_count = QRY // span_len
    grouped = query_points.reshape(PARAMS, span_count, span_len).transpose(1, 0, 2)

    def predict_block(query_block):
        return jnp.dot(weights_low, kernel_values(train_inputs, query_block, inv_length), preferred_element_type=jnp.float32)
    blocks_out = lax.map(predict_block, grouped)
    predicted_mean = blocks_out.transpose(1, 0, 2).reshape(M, QRY) * amplitude[:, None]
    return (weights, predicted_mean)
```

```python
import functools
import math

import jax
import jax.numpy as jnp
from jax import lax
from jax.experimental import pallas as pl
from jax.experimental.pallas import tpu as pltpu
from jax.sharding import PartitionSpec as P

CHUNKS = 2
LOG2E = math.log2(math.e)
EPSILON = 1e-06 * LOG2E * LOG2E
BF16 = jnp.bfloat16
F32 = jnp.float32
SEND_TYPE = jnp.float32


def split_two(x):
    high = x.astype(BF16)
    return high, (x - high.astype(F32)).astype(BF16)


def split_three(x):
    first = x.astype(BF16).astype(F32)
    rest = x - first
    second = rest.astype(BF16).astype(F32)
    third = (rest - second).astype(BF16).astype(F32)
    return first, second, third


def product(x, high, low):
    x_high, x_low = split_two(x)
    rows = x.shape[0]
    both = jnp.dot(
        jnp.concatenate([x_high, x_low], axis=0), high, preferred_element_type=F32
    )
    return both[:rows] + (both[rows:] + jnp.dot(x_high, low, preferred_element_type=F32))


def scaled_points(points, scale):
    params, count = points.shape
    padded = -(-params // 16) * 16
    x = (points - 0.5) * scale[:params]
    return jnp.concatenate([x, jnp.zeros((padded - params, count), F32)], axis=0)


def norm_rows(x, ones_first):
    count = x.shape[1]
    n1, n2, n3 = split_three(jnp.sum(x * x, axis=0, keepdims=True))
    row = lax.broadcasted_iota(jnp.int32, (16, count), 0)
    at = 3 if ones_first else 0
    one_at = 0 if ones_first else 3
    out = jnp.where((row >= one_at) & (row < one_at + 3), 1.0, 0.0)
    out = jnp.where(row == at, n1, out)
    out = jnp.where(row == at + 1, n2, out)
    return jnp.where(row == at + 2, n3, out)


def kernel(
    rows,
    inv_ref,
    c_hbm,
    f_hbm,
    b_hbm,
    t_hbm,
    q_hbm,
    w_hbm,
    p_hbm,
    c_buf,
    f1_buf,
    f0_buf,
    b_buf,
    q_buf,
    t_all,
    h1_buf,
    l1_buf,
    h2_buf,
    l2_buf,
    part1,
    part0,
    got1,
    got0,
    got_t,
    w_buf,
    w_all,
    a_t,
    q_aug,
    k_all,
    acc,
    local_sem,
    t_send,
    t_recv,
    p1_send,
    p1_recv,
    p0_send,
    p0_recv,
    tt_send,
    tt_recv,
    c_send,
    c_recv,
    w_send,
    w_recv,
    out_sem,
):
    me = lax.axis_index("rows")
    m, block = c_buf.shape
    params, width = q_buf.shape
    step = m // CHUNKS
    tile = 512 if width % 512 == 0 else width
    tiles = width // tile

    def load(src, dst, at):
        copy = pltpu.make_async_copy(src, dst, local_sem.at[at])
        copy.start()
        return copy

    def remote(src, dst, send, recv, peer):
        return pltpu.make_async_remote_copy(
            src_ref=src,
            dst_ref=dst,
            send_sem=send,
            recv_sem=recv,
            device_id={"rows": peer},
            device_id_type=pl.DeviceIdType.MESH,
        )

    in_c = load(c_hbm, c_buf, 0)
    in_f1 = load(f_hbm.at[:, pl.ds(block, block)], f1_buf, 1)
    in_t = load(t_hbm, t_all.at[me], 2)
    in_q = load(q_hbm.at[:, pl.ds(pl.multiple_of(me * width, 128), width)], q_buf, 3)
    in_f0 = load(f_hbm.at[:, pl.ds(0, block)], f0_buf, 4)
    in_b = load(b_hbm, b_buf, 5)

    barrier = pltpu.get_barrier_semaphore()
    for k in range(1, rows):
        pl.semaphore_signal(
            barrier,
            inc=1,
            device_id={"rows": lax.rem(me + k, rows)},
            device_id_type=pl.DeviceIdType.MESH,
        )
    pl.semaphore_wait(barrier, rows - 1)

    def t_copy(k):
        return remote(
            t_hbm, t_all.at[me], t_send.at[k - 1], t_recv.at[me], lax.rem(me + k, rows)
        )

    for k in range(1, rows):
        t_copy(k).start()

    def chunk(c):
        return pl.ds(c * step, step)

    def p1_copy(c, slot):
        return remote(
            part1.at[chunk(c)],
            got1.at[slot, chunk(c)],
            p1_send.at[c],
            p1_recv.at[slot, c],
            1,
        )

    def p0_copy(c, slot):
        return remote(
            part0.at[chunk(c)],
            got0.at[slot, chunk(c)],
            p0_send.at[c],
            p0_recv.at[slot, c],
            0,
        )

    def tt_copy(c):
        return remote(
            part0.at[chunk(c)], got_t.at[chunk(c)], tt_send.at[c], tt_recv.at[c], 0
        )

    def c_copy(k):
        return remote(
            w_all.at[me],
            w_all.at[me],
            c_send.at[k - 1],
            c_recv.at[me],
            lax.rem(me + k, rows),
        )

    def w_copy(c, k):
        return remote(
            w_all.at[me, chunk(c)],
            w_all.at[me, chunk(c)],
            w_send.at[c, k - 1],
            w_recv.at[me, c],
            lax.rem(me + k, rows),
        )

    in_c.wait()
    in_f1.wait()

    @pl.when(me >= 2)
    def _():
        h1_buf[...], l1_buf[...] = split_two(f1_buf[...])
        for c in range(CHUNKS):
            part1[chunk(c)] = product(c_buf[chunk(c)], h1_buf[...], l1_buf[...]).astype(SEND_TYPE)
            p1_copy(c, me - 2).start()
        w_all[me] = c_buf[...].astype(BF16)
        for k in range(1, rows):
            c_copy(k).start()

    in_f0.wait()
    in_b.wait()
    h2_buf[...], l2_buf[...] = split_two(f0_buf[...])

    @pl.when(me >= 2)
    def _():
        for c in range(CHUNKS):
            part0[chunk(c)] = product(c_buf[chunk(c)], h2_buf[...], l2_buf[...]).astype(SEND_TYPE)
            p0_copy(c, me - 2).start()

    @pl.when(me < 2)
    def _():
        h1_buf[...], l1_buf[...] = split_two(b_buf[...])

    row = lax.broadcasted_iota(jnp.int32, (params, 1), 0)
    scale = jnp.zeros((params, 1), F32)
    for d in range(params):
        scale = jnp.where(row == d, inv_ref[d] * LOG2E, scale)
    in_q.wait()
    x = scaled_points(q_buf[...], scale)
    x1, x2, x3 = split_three(-2.0 * x)
    pieces = [x1, x2, x1, x3, x2, x1, norm_rows(x, True)]
    used = sum(piece.shape[0] for piece in pieces)
    depth = q_aug.shape[0]
    if depth > used:
        pieces.append(jnp.zeros((depth - used, width), F32))
    q_aug[...] = jnp.concatenate(pieces, axis=0).astype(BF16)

    def train_side(r):
        @pl.when(r == me)
        def _():
            in_t.wait()

        @pl.when(r != me)
        def _():
            remote(t_hbm, t_all.at[r], t_send.at[0], t_recv.at[r], 0).wait_recv()

        y = scaled_points(t_all[r], scale)
        y1, y2, y3 = split_three(y)
        parts = [y1, y1, y2, y1, y2, y3, norm_rows(y, False)]
        if depth > used:
            parts.append(jnp.zeros((depth - used, block), F32))
        a_t[...] = jnp.concatenate(parts, axis=0).T.astype(BF16)

    def kernel_tile(j):
        at = pl.ds(pl.multiple_of(j * tile, 128), tile)
        y = jnp.dot(a_t[...], q_aug[:, at], preferred_element_type=F32)
        y = jnp.maximum(y + EPSILON, EPSILON)
        return at, jnp.exp2(-(y * lax.rsqrt(y))).astype(BF16)

    for r in range(2):
        train_side(r)

        def store_tile(j, carry, r=r):
            at, values = kernel_tile(j)
            k_all[r, :, at] = values
            return carry

        lax.fori_loop(0, tiles, store_tile, 0)

    def out_copy(c):
        return pltpu.make_async_copy(w_buf.at[chunk(c)], w_hbm.at[chunk(c)], out_sem.at[c])

    @pl.when(me == 1)
    def _():
        for c in range(CHUNKS):
            rest = jnp.zeros((step, block), F32)
            for s in range(rows - 2):
                p1_copy(c, s).wait_recv()
                rest = rest + got1[s, chunk(c)].astype(F32)
            value = product(c_buf[chunk(c)] - rest, h1_buf[...], l1_buf[...])
            w_buf[chunk(c)] = value
            part0[chunk(c)] = product(value, h2_buf[...], l2_buf[...]).astype(SEND_TYPE)
            tt_copy(c).start()
            w_all[1, chunk(c)] = value.astype(BF16)
            for k in range(1, rows):
                w_copy(c, k).start()
            out_copy(c).start()

    acc[...] = jnp.zeros_like(acc)

    def later_block(r, carry):
        train_side(r)

        @pl.when(r != me)
        def _():
            remote(w_all.at[r], w_all.at[r], c_send.at[0], c_recv.at[r], 0).wait_recv()

        def add_tile(j, inner):
            at, values = kernel_tile(j)
            acc[:, at] += jnp.dot(w_all[r], values, preferred_element_type=F32)
            return inner

        return lax.fori_loop(0, tiles, add_tile, carry)

    lax.fori_loop(2, rows, later_block, 0)

    @pl.when(me == 0)
    def _():
        for c in range(CHUNKS):
            rest = jnp.zeros((step, block), F32)
            for s in range(rows - 2):
                p0_copy(c, s).wait_recv()
                rest = rest + got0[s, chunk(c)].astype(F32)
            tt_copy(c).wait_recv()
            rest = rest + got_t[chunk(c)].astype(F32)
            value = product(c_buf[chunk(c)] - rest, h1_buf[...], l1_buf[...])
            w_buf[chunk(c)] = value
            w_all[0, chunk(c)] = value.astype(BF16)
            for k in range(1, rows):
                w_copy(c, k).start()
            out_copy(c).start()

    def w_wait(r):
        @pl.when(me != r)
        def _():
            for c in range(CHUNKS):
                remote(
                    w_all.at[r, chunk(c)],
                    w_all.at[r, chunk(c)],
                    w_send.at[c, 0],
                    w_recv.at[r, c],
                    0,
                ).wait_recv()

    w_wait(1)

    def add_one(j, carry):
        at = pl.ds(pl.multiple_of(j * tile, 128), tile)
        acc[:, at] += jnp.dot(w_all[1], k_all[1, :, at], preferred_element_type=F32)
        return carry

    lax.fori_loop(0, tiles, add_one, 0)
    w_wait(0)

    def done_copy(j):
        at = pl.ds(j * tile, tile)
        return pltpu.make_async_copy(acc.at[:, at], p_hbm.at[:, at], out_sem.at[CHUNKS + j])

    for j in range(tiles):
        at = pl.ds(j * tile, tile)
        acc[:, at] += jnp.dot(w_all[0], k_all[0, :, at], preferred_element_type=F32)
        done_copy(j).start()

    for k in range(1, rows):
        t_copy(k).wait_send()

    @pl.when(me >= 2)
    def _():
        for c in range(CHUNKS):
            p1_copy(c, me - 2).wait_send()
            p0_copy(c, me - 2).wait_send()
        for k in range(1, rows):
            c_copy(k).wait_send()

    @pl.when(me == 1)
    def _():
        for c in range(CHUNKS):
            tt_copy(c).wait_send()

    @pl.when(me < 2)
    def _():
        for c in range(CHUNKS):
            for k in range(1, rows):
                w_copy(c, k).wait_send()
            out_copy(c).wait()

    for j in range(tiles):
        done_copy(j).wait()


def on_device(
    coefficients, factor_panel, block_inverse, train_inputs, query_points, inv_length, amplitude
):
    rows = lax.axis_size("rows")
    m, block = coefficients.shape
    params = train_inputs.shape[0]
    width = query_points.shape[1] // rows
    padded = -(-params // 16) * 16
    depth = -(-(6 * padded + 16) // 128) * 128
    tile = 512 if width % 512 == 0 else width
    anywhere = pl.BlockSpec(memory_space=pl.ANY)
    dma = pltpu.SemaphoreType.DMA
    vmem = pltpu.VMEM
    solved, summed = pl.pallas_call(
        functools.partial(kernel, rows),
        out_shape=(
            jax.ShapeDtypeStruct((m, block), F32),
            jax.ShapeDtypeStruct((m, width), F32),
        ),
        in_specs=[pl.BlockSpec(memory_space=pltpu.SMEM)] + [anywhere] * 5,
        out_specs=(anywhere, anywhere),
        scratch_shapes=[
            vmem((m, block), F32),
            vmem((block, block), F32),
            vmem((block, block), F32),
            vmem((block, block), F32),
            vmem((params, width), F32),
            vmem((rows, params, block), F32),
            vmem((block, block), BF16),
            vmem((block, block), BF16),
            vmem((block, block), BF16),
            vmem((block, block), BF16),
            vmem((m, block), SEND_TYPE),
            vmem((m, block), SEND_TYPE),
            vmem((rows - 2, m, block), SEND_TYPE),
            vmem((rows - 2, m, block), SEND_TYPE),
            vmem((m, block), SEND_TYPE),
            vmem((m, block), F32),
            vmem((rows, m, block), BF16),
            vmem((block, depth), BF16),
            vmem((depth, width), BF16),
            vmem((2, block, width), BF16),
            vmem((m, width), F32),
            dma((6,)),
            dma((rows - 1,)),
            dma((rows,)),
            dma((CHUNKS,)),
            dma((rows - 2, CHUNKS)),
            dma((CHUNKS,)),
            dma((rows - 2, CHUNKS)),
            dma((CHUNKS,)),
            dma((CHUNKS,)),
            dma((rows - 1,)),
            dma((rows,)),
            dma((CHUNKS, rows - 1)),
            dma((2, CHUNKS)),
            dma((CHUNKS + width // tile,)),
        ],
        compiler_params=pltpu.CompilerParams(
            collective_id=0, has_side_effects=True, vmem_limit_bytes=48 * 1024 * 1024
        ),
    )(inv_length, coefficients, factor_panel, block_inverse, train_inputs, query_points)
    weights = jnp.where(lax.axis_index("rows") < 2, solved, coefficients)
    return (weights, summed * amplitude[:, None])


def solution(mesh):
    return jax.shard_map(
        on_device,
        mesh=mesh,
        in_specs=(
            P("cols", "rows"),
            P("rows", None),
            P("rows", None),
            P(None, "rows"),
            P(),
            P(),
            P("cols"),
        ),
        out_specs=(P("cols", "rows"), P("cols", "rows")),
        check_vma=False,
    )
```

```python
import functools
import math

import jax
import jax.numpy as jnp
from jax import lax
from jax.experimental import pallas as pl
from jax.experimental.pallas import tpu as pltpu
from jax.sharding import PartitionSpec as P

CHUNKS = 4
LOG2E = math.log2(math.e)
EPSILON = 1e-06 * LOG2E * LOG2E
BF16 = jnp.bfloat16
F32 = jnp.float32
SEND_TYPE = jnp.bfloat16


def split_two(x):
    high = x.astype(BF16)
    return high, (x - high.astype(F32)).astype(BF16)


def split_three(x):
    first = x.astype(BF16).astype(F32)
    rest = x - first
    second = rest.astype(BF16).astype(F32)
    third = (rest - second).astype(BF16).astype(F32)
    return first, second, third


def product(x, high, low):
    x_high, x_low = split_two(x)
    rows = x.shape[0]
    both = jnp.dot(
        jnp.concatenate([x_high, x_low], axis=0), high, preferred_element_type=F32
    )
    return both[:rows] + (both[rows:] + jnp.dot(x_high, low, preferred_element_type=F32))


def scaled_points(points, scale):
    params, count = points.shape
    padded = -(-params // 16) * 16
    x = (points - 0.5) * scale[:params]
    return jnp.concatenate([x, jnp.zeros((padded - params, count), F32)], axis=0)


def norm_rows(x, ones_first):
    count = x.shape[1]
    n1, n2, n3 = split_three(jnp.sum(x * x, axis=0, keepdims=True))
    row = lax.broadcasted_iota(jnp.int32, (16, count), 0)
    at = 3 if ones_first else 0
    one_at = 0 if ones_first else 3
    out = jnp.where((row >= one_at) & (row < one_at + 3), 1.0, 0.0)
    out = jnp.where(row == at, n1, out)
    out = jnp.where(row == at + 1, n2, out)
    return jnp.where(row == at + 2, n3, out)


def kernel(
    rows,
    inv_ref,
    c_hbm,
    f_hbm,
    b_hbm,
    t_hbm,
    q_hbm,
    w_hbm,
    p_hbm,
    c_buf,
    f1_buf,
    f0_buf,
    b_buf,
    q_buf,
    t_all,
    h1_buf,
    l1_buf,
    h2_buf,
    l2_buf,
    part1,
    part0,
    got1,
    got0,
    got_t,
    w_buf,
    w_all,
    a_t,
    q_aug,
    k_all,
    acc,
    local_sem,
    t_send,
    t_recv,
    p1_send,
    p1_recv,
    p0_send,
    p0_recv,
    tt_send,
    tt_recv,
    c_send,
    c_recv,
    w_send,
    w_recv,
    out_sem,
):
    me = lax.axis_index("rows")
    m, block = c_buf.shape
    params, width = q_buf.shape
    step = m // CHUNKS
    tile = 512 if width % 512 == 0 else width
    tiles = width // tile

    def load(src, dst, at):
        copy = pltpu.make_async_copy(src, dst, local_sem.at[at])
        copy.start()
        return copy

    def remote(src, dst, send, recv, peer):
        return pltpu.make_async_remote_copy(
            src_ref=src,
            dst_ref=dst,
            send_sem=send,
            recv_sem=recv,
            device_id={"rows": peer},
            device_id_type=pl.DeviceIdType.MESH,
        )

    in_c = load(c_hbm, c_buf, 0)
    in_f1 = load(f_hbm.at[:, pl.ds(block, block)], f1_buf, 1)
    in_t = load(t_hbm, t_all.at[me], 2)
    in_q = load(q_hbm.at[:, pl.ds(pl.multiple_of(me * width, 128), width)], q_buf, 3)
    in_f0 = load(f_hbm.at[:, pl.ds(0, block)], f0_buf, 4)
    in_b = load(b_hbm, b_buf, 5)

    barrier = pltpu.get_barrier_semaphore()
    for k in range(1, rows):
        pl.semaphore_signal(
            barrier,
            inc=1,
            device_id={"rows": lax.rem(me + k, rows)},
            device_id_type=pl.DeviceIdType.MESH,
        )
    pl.semaphore_wait(barrier, rows - 1)

    def t_copy(k):
        return remote(
            t_hbm, t_all.at[me], t_send.at[k - 1], t_recv.at[me], lax.rem(me + k, rows)
        )

    for k in range(1, rows):
        t_copy(k).start()

    def chunk(c):
        return pl.ds(c * step, step)

    def p1_copy(c, slot):
        return remote(
            part1.at[chunk(c)],
            got1.at[slot, chunk(c)],
            p1_send.at[c],
            p1_recv.at[slot, c],
            1,
        )

    def p0_copy(c, slot):
        return remote(
            part0.at[chunk(c)],
            got0.at[slot, chunk(c)],
            p0_send.at[c],
            p0_recv.at[slot, c],
            0,
        )

    def tt_copy(c):
        return remote(
            part0.at[chunk(c)], got_t.at[chunk(c)], tt_send.at[c], tt_recv.at[c], 0
        )

    def c_copy(k):
        return remote(
            w_all.at[me],
            w_all.at[me],
            c_send.at[k - 1],
            c_recv.at[me],
            lax.rem(me + k, rows),
        )

    def w_copy(c, k):
        return remote(
            w_all.at[me, chunk(c)],
            w_all.at[me, chunk(c)],
            w_send.at[c, k - 1],
            w_recv.at[me, c],
            lax.rem(me + k, rows),
        )

    in_c.wait()
    in_f1.wait()

    @pl.when(me >= 2)
    def _():
        h1_buf[...], l1_buf[...] = split_two(f1_buf[...])
        for half in range(2):
            at = pl.ds(half * m // 2, m // 2)
            part1[at] = product(c_buf[at], h1_buf[...], l1_buf[...]).astype(SEND_TYPE)
            for c in range(half * CHUNKS // 2, (half + 1) * CHUNKS // 2):
                p1_copy(c, me - 2).start()
        w_all[me] = c_buf[...].astype(BF16)

    in_f0.wait()
    in_b.wait()
    h2_buf[...], l2_buf[...] = split_two(f0_buf[...])

    @pl.when(me >= 2)
    def _():
        part0[...] = product(c_buf[...], h2_buf[...], l2_buf[...]).astype(SEND_TYPE)
        for c in range(CHUNKS):
            p0_copy(c, me - 2).start()

    @pl.when(me < 2)
    def _():
        h1_buf[...], l1_buf[...] = split_two(b_buf[...])

    row = lax.broadcasted_iota(jnp.int32, (params, 1), 0)
    scale = jnp.zeros((params, 1), F32)
    for d in range(params):
        scale = jnp.where(row == d, inv_ref[d] * LOG2E, scale)
    in_q.wait()
    x = scaled_points(q_buf[...], scale)
    x1, x2, x3 = split_three(-2.0 * x)
    pieces = [x1, x2, x1, x3, x2, x1, norm_rows(x, True)]
    used = sum(piece.shape[0] for piece in pieces)
    depth = q_aug.shape[0]
    if depth > used:
        pieces.append(jnp.zeros((depth - used, width), F32))
    q_aug[...] = jnp.concatenate(pieces, axis=0).astype(BF16)

    def train_side(r):
        @pl.when(r == me)
        def _():
            in_t.wait()

        @pl.when(r != me)
        def _():
            remote(t_hbm, t_all.at[r], t_send.at[0], t_recv.at[r], 0).wait_recv()

        y = scaled_points(t_all[r], scale)
        y1, y2, y3 = split_three(y)
        parts = [y1, y1, y2, y1, y2, y3, norm_rows(y, False)]
        if depth > used:
            parts.append(jnp.zeros((depth - used, block), F32))
        a_t[...] = jnp.concatenate(parts, axis=0).T.astype(BF16)

    def kernel_tile(j):
        at = pl.ds(pl.multiple_of(j * tile, 128), tile)
        y = jnp.dot(a_t[...], q_aug[:, at], preferred_element_type=F32)
        y = jnp.maximum(y + EPSILON, EPSILON)
        return at, jnp.exp2(-(y * lax.rsqrt(y))).astype(BF16)

    def kernel_block(r, carry):
        train_side(r)

        def store_tile(j, inner):
            at, values = kernel_tile(j)
            k_all[r, :, at] = values
            return inner

        return lax.fori_loop(0, tiles, store_tile, carry)

    lax.fori_loop(0, 2, kernel_block, 0)

    @pl.when(me >= 2)
    def _():
        for k in range(1, rows):
            c_copy(k).start()

    def out_copy(c):
        return pltpu.make_async_copy(w_buf.at[chunk(c)], w_hbm.at[chunk(c)], out_sem.at[c])

    @pl.when(me == 1)
    def _():
        for c in range(CHUNKS):
            rest = jnp.zeros((step, block), F32)
            for s in range(rows - 2):
                p1_copy(c, s).wait_recv()
                rest = rest + got1[s, chunk(c)].astype(F32)
            value = product(c_buf[chunk(c)] - rest, h1_buf[...], l1_buf[...])
            w_buf[chunk(c)] = value
            part0[chunk(c)] = product(value, h2_buf[...], l2_buf[...]).astype(SEND_TYPE)
            tt_copy(c).start()
            w_all[1, chunk(c)] = value.astype(BF16)
            out_copy(c).start()
        for c in range(CHUNKS):
            for k in range(1, rows):
                w_copy(c, k).start()

    lax.fori_loop(2, rows, kernel_block, 0)

    @pl.when(me == 0)
    def _():
        for c in range(CHUNKS):
            rest = jnp.zeros((step, block), F32)
            for s in range(rows - 2):
                p0_copy(c, s).wait_recv()
                rest = rest + got0[s, chunk(c)].astype(F32)
            tt_copy(c).wait_recv()
            rest = rest + got_t[chunk(c)].astype(F32)
            value = product(c_buf[chunk(c)] - rest, h1_buf[...], l1_buf[...])
            w_buf[chunk(c)] = value
            w_all[0, chunk(c)] = value.astype(BF16)
            for k in range(1, rows):
                w_copy(c, k).start()
            out_copy(c).start()

    acc[...] = jnp.zeros_like(acc)

    def add_block(r):
        def add_tile(j, carry):
            at = pl.ds(pl.multiple_of(j * tile, 128), tile)
            acc[:, at] += jnp.dot(w_all[r], k_all[r, :, at], preferred_element_type=F32)
            return carry

        lax.fori_loop(0, tiles, add_tile, 0)

    def later_block(r, carry):
        @pl.when(r != me)
        def _():
            remote(w_all.at[r], w_all.at[r], c_send.at[0], c_recv.at[r], 0).wait_recv()

        add_block(r)
        return carry

    lax.fori_loop(2, rows, later_block, 0)

    def w_wait(r):
        @pl.when(me != r)
        def _():
            for c in range(CHUNKS):
                remote(
                    w_all.at[r, chunk(c)],
                    w_all.at[r, chunk(c)],
                    w_send.at[c, 0],
                    w_recv.at[r, c],
                    0,
                ).wait_recv()

    w_wait(1)

    add_block(1)
    w_wait(0)

    def done_copy(j):
        at = pl.ds(j * tile, tile)
        return pltpu.make_async_copy(acc.at[:, at], p_hbm.at[:, at], out_sem.at[CHUNKS + j])

    for j in range(tiles):
        at = pl.ds(j * tile, tile)
        acc[:, at] += jnp.dot(w_all[0], k_all[0, :, at], preferred_element_type=F32)
        done_copy(j).start()

    for k in range(1, rows):
        t_copy(k).wait_send()

    @pl.when(me >= 2)
    def _():
        for c in range(CHUNKS):
            p1_copy(c, me - 2).wait_send()
            p0_copy(c, me - 2).wait_send()
        for k in range(1, rows):
            c_copy(k).wait_send()

    @pl.when(me == 1)
    def _():
        for c in range(CHUNKS):
            tt_copy(c).wait_send()

    @pl.when(me < 2)
    def _():
        for c in range(CHUNKS):
            for k in range(1, rows):
                w_copy(c, k).wait_send()
            out_copy(c).wait()

    for j in range(tiles):
        done_copy(j).wait()


def on_device(
    coefficients, factor_panel, block_inverse, train_inputs, query_points, inv_length, amplitude
):
    rows = lax.axis_size("rows")
    m, block = coefficients.shape
    params = train_inputs.shape[0]
    width = query_points.shape[1] // rows
    padded = -(-params // 16) * 16
    depth = -(-(6 * padded + 16) // 128) * 128
    tile = 512 if width % 512 == 0 else width
    anywhere = pl.BlockSpec(memory_space=pltpu.HBM)
    dma = pltpu.SemaphoreType.DMA
    vmem = pltpu.VMEM
    solved, summed = pl.pallas_call(
        functools.partial(kernel, rows),
        out_shape=(
            jax.ShapeDtypeStruct((m, block), F32),
            jax.ShapeDtypeStruct((m, width), F32),
        ),
        in_specs=[pl.BlockSpec(memory_space=pltpu.SMEM)] + [anywhere] * 5,
        out_specs=(anywhere, anywhere),
        scratch_shapes=[
            vmem((m, block), F32),
            vmem((block, block), F32),
            vmem((block, block), F32),
            vmem((block, block), F32),
            vmem((params, width), F32),
            vmem((rows, params, block), F32),
            vmem((block, block), BF16),
            vmem((block, block), BF16),
            vmem((block, block), BF16),
            vmem((block, block), BF16),
            vmem((m, block), SEND_TYPE),
            vmem((m, block), SEND_TYPE),
            vmem((rows - 2, m, block), SEND_TYPE),
            vmem((rows - 2, m, block), SEND_TYPE),
            vmem((m, block), SEND_TYPE),
            vmem((m, block), F32),
            vmem((rows, m, block), BF16),
            vmem((block, depth), BF16),
            vmem((depth, width), BF16),
            vmem((rows, block, width), BF16),
            vmem((m, width), F32),
            dma((6,)),
            dma((rows - 1,)),
            dma((rows,)),
            dma((CHUNKS,)),
            dma((rows - 2, CHUNKS)),
            dma((CHUNKS,)),
            dma((rows - 2, CHUNKS)),
            dma((CHUNKS,)),
            dma((CHUNKS,)),
            dma((rows - 1,)),
            dma((rows,)),
            dma((CHUNKS, rows - 1)),
            dma((2, CHUNKS)),
            dma((CHUNKS + width // tile,)),
        ],
        compiler_params=pltpu.CompilerParams(
            collective_id=0, has_side_effects=True, vmem_limit_bytes=60 * 1024 * 1024
        ),
    )(inv_length, coefficients, factor_panel, block_inverse, train_inputs, query_points)
    weights = jnp.where(lax.axis_index("rows") < 2, solved, coefficients)
    return (weights, summed * amplitude[:, None])


def solution(mesh):
    return jax.shard_map(
        on_device,
        mesh=mesh,
        in_specs=(
            P("cols", "rows"),
            P("rows", None),
            P("rows", None),
            P(None, "rows"),
            P(),
            P(),
            P("cols"),
        ),
        out_specs=(P("cols", "rows"), P("cols", "rows")),
        check_vma=False,
    )
```

```python
import functools
import math

import jax
import jax.numpy as jnp
from jax import lax
from jax.experimental import pallas as pl
from jax.experimental.pallas import tpu as pltpu
from jax.sharding import PartitionSpec as P

CHUNKS = 4
LOG2E = math.log2(math.e)
EPSILON = 1e-06 * LOG2E * LOG2E
BF16 = jnp.bfloat16
F32 = jnp.float32
SEND_TYPE = jnp.bfloat16


def split_two(x):
    high = x.astype(BF16)
    return high, (x - high.astype(F32)).astype(BF16)


def split_three(x):
    first = x.astype(BF16).astype(F32)
    rest = x - first
    second = rest.astype(BF16).astype(F32)
    third = (rest - second).astype(BF16).astype(F32)
    return first, second, third


def product(x, high, low):
    x_high, x_low = split_two(x)
    rows = x.shape[0]
    both = jnp.dot(
        jnp.concatenate([x_high, x_low], axis=0), high, preferred_element_type=F32
    )
    return both[:rows] + (both[rows:] + jnp.dot(x_high, low, preferred_element_type=F32))


def scaled_points(points, scale):
    params, count = points.shape
    padded = -(-params // 16) * 16
    x = (points - 0.5) * scale[:params]
    return jnp.concatenate([x, jnp.zeros((padded - params, count), F32)], axis=0)


def norm_rows(x, ones_first):
    count = x.shape[1]
    n1, n2, n3 = split_three(jnp.sum(x * x, axis=0, keepdims=True))
    row = lax.broadcasted_iota(jnp.int32, (16, count), 0)
    at = 3 if ones_first else 0
    one_at = 0 if ones_first else 3
    out = jnp.where((row >= one_at) & (row < one_at + 3), 1.0, 0.0)
    out = jnp.where(row == at, n1, out)
    out = jnp.where(row == at + 1, n2, out)
    return jnp.where(row == at + 2, n3, out)


def kernel(
    rows,
    inv_ref,
    c_hbm,
    f_hbm,
    b_hbm,
    t_hbm,
    q_hbm,
    w_buf,
    acc,
    c_buf,
    f1_buf,
    f0_buf,
    b_buf,
    q_buf,
    t_all,
    h1_buf,
    l1_buf,
    h2_buf,
    l2_buf,
    part1,
    part0,
    got1,
    got0,
    got_t,
    w_all,
    a_t,
    q_aug,
    k_all,
    local_sem,
    t_send,
    t_recv,
    p1_send,
    p1_recv,
    p0_send,
    p0_recv,
    tt_send,
    tt_recv,
    c_send,
    c_recv,
    w_send,
    w_recv,
):
    me = lax.axis_index("rows")
    m, block = c_buf.shape
    params, width = q_buf.shape
    step = m // CHUNKS
    tile = 512 if width % 512 == 0 else width
    tiles = width // tile

    def load(src, dst, at):
        copy = pltpu.make_async_copy(src, dst, local_sem.at[at])
        copy.start()
        return copy

    def remote(src, dst, send, recv, peer):
        return pltpu.make_async_remote_copy(
            src_ref=src,
            dst_ref=dst,
            send_sem=send,
            recv_sem=recv,
            device_id={"rows": peer},
            device_id_type=pl.DeviceIdType.MESH,
        )

    in_c = load(c_hbm, c_buf, 0)
    in_f1 = load(f_hbm.at[:, pl.ds(block, block)], f1_buf, 1)
    in_t = load(t_hbm, t_all.at[me], 2)
    in_q = load(q_hbm.at[:, pl.ds(pl.multiple_of(me * width, 128), width)], q_buf, 3)
    in_f0 = load(f_hbm.at[:, pl.ds(0, block)], f0_buf, 4)
    in_b = load(b_hbm, b_buf, 5)

    barrier = pltpu.get_barrier_semaphore()
    for k in range(1, rows):
        pl.semaphore_signal(
            barrier,
            inc=1,
            device_id={"rows": lax.rem(me + k, rows)},
            device_id_type=pl.DeviceIdType.MESH,
        )
    pl.semaphore_wait(barrier, rows - 1)

    def t_copy(k):
        return remote(
            t_hbm, t_all.at[me], t_send.at[k - 1], t_recv.at[me], lax.rem(me + k, rows)
        )

    for k in range(1, rows):
        t_copy(k).start()

    def chunk(c):
        return pl.ds(c * step, step)

    def p1_copy(c, slot):
        return remote(
            part1.at[chunk(c)],
            got1.at[slot, chunk(c)],
            p1_send.at[c],
            p1_recv.at[slot, c],
            1,
        )

    def p0_copy(c, slot):
        return remote(
            part0.at[chunk(c)],
            got0.at[slot, chunk(c)],
            p0_send.at[c],
            p0_recv.at[slot, c],
            0,
        )

    def tt_copy(c):
        return remote(
            part0.at[chunk(c)], got_t.at[chunk(c)], tt_send.at[c], tt_recv.at[c], 0
        )

    def c_copy(k):
        return remote(
            w_all.at[me],
            w_all.at[me],
            c_send.at[k - 1],
            c_recv.at[me],
            lax.rem(me + k, rows),
        )

    def w_copy(c, k):
        return remote(
            w_all.at[me, chunk(c)],
            w_all.at[me, chunk(c)],
            w_send.at[c, k - 1],
            w_recv.at[me, c],
            lax.rem(me + k, rows),
        )

    in_c.wait()
    in_f1.wait()

    @pl.when(me >= 2)
    def _():
        h1_buf[...], l1_buf[...] = split_two(f1_buf[...])
        for half in range(2):
            at = pl.ds(half * m // 2, m // 2)
            part1[at] = product(c_buf[at], h1_buf[...], l1_buf[...]).astype(SEND_TYPE)
            for c in range(half * CHUNKS // 2, (half + 1) * CHUNKS // 2):
                p1_copy(c, me - 2).start()
        w_all[me] = c_buf[...].astype(BF16)

    in_f0.wait()
    in_b.wait()
    h2_buf[...], l2_buf[...] = split_two(f0_buf[...])

    @pl.when(me >= 2)
    def _():
        part0[...] = product(c_buf[...], h2_buf[...], l2_buf[...]).astype(SEND_TYPE)
        for c in range(CHUNKS):
            p0_copy(c, me - 2).start()

    @pl.when(me < 2)
    def _():
        h1_buf[...], l1_buf[...] = split_two(b_buf[...])

    row = lax.broadcasted_iota(jnp.int32, (params, 1), 0)
    scale = jnp.zeros((params, 1), F32)
    for d in range(params):
        scale = jnp.where(row == d, inv_ref[d] * LOG2E, scale)
    in_q.wait()
    x = scaled_points(q_buf[...], scale)
    x1, x2, x3 = split_three(-2.0 * x)
    pieces = [x1, x2, x1, x3, x2, x1, norm_rows(x, True)]
    used = sum(piece.shape[0] for piece in pieces)
    depth = q_aug.shape[0]
    if depth > used:
        pieces.append(jnp.zeros((depth - used, width), F32))
    q_aug[...] = jnp.concatenate(pieces, axis=0).astype(BF16)

    def train_side(r):
        @pl.when(r == me)
        def _():
            in_t.wait()

        @pl.when(r != me)
        def _():
            remote(t_hbm, t_all.at[r], t_send.at[0], t_recv.at[r], 0).wait_recv()

        y = scaled_points(t_all[r], scale)
        y1, y2, y3 = split_three(y)
        parts = [y1, y1, y2, y1, y2, y3, norm_rows(y, False)]
        if depth > used:
            parts.append(jnp.zeros((depth - used, block), F32))
        a_t[...] = jnp.concatenate(parts, axis=0).T.astype(BF16)

    def kernel_tile(j):
        at = pl.ds(pl.multiple_of(j * tile, 128), tile)
        y = jnp.dot(a_t[...], q_aug[:, at], preferred_element_type=F32)
        y = jnp.maximum(y + EPSILON, EPSILON)
        return at, jnp.exp2(-(y * lax.rsqrt(y))).astype(BF16)

    def kernel_block(r, carry):
        train_side(r)

        def store_tile(j, inner):
            at, values = kernel_tile(j)
            k_all[r, :, at] = values
            return inner

        return lax.fori_loop(0, tiles, store_tile, carry)

    lax.fori_loop(0, 2, kernel_block, 0)

    @pl.when(me >= 2)
    def _():
        for k in range(1, rows):
            c_copy(k).start()

    @pl.when(me == 1)
    def _():
        for c in range(CHUNKS):
            rest = jnp.zeros((step, block), F32)
            for s in range(rows - 2):
                p1_copy(c, s).wait_recv()
                rest = rest + got1[s, chunk(c)].astype(F32)
            value = product(c_buf[chunk(c)] - rest, h1_buf[...], l1_buf[...])
            w_buf[chunk(c)] = value
            part0[chunk(c)] = product(value, h2_buf[...], l2_buf[...]).astype(SEND_TYPE)
            tt_copy(c).start()
            w_all[1, chunk(c)] = value.astype(BF16)
        for c in range(CHUNKS):
            for k in range(1, rows):
                w_copy(c, k).start()

    lax.fori_loop(2, rows, kernel_block, 0)

    acc[...] = jnp.zeros_like(acc)

    def add_block(r):
        def add_tile(j, carry):
            at = pl.ds(pl.multiple_of(j * tile, 128), tile)
            acc[:, at] += jnp.dot(w_all[r], k_all[r, :, at], preferred_element_type=F32)
            return carry

        lax.fori_loop(0, tiles, add_tile, 0)

    def later_block(r, carry):
        @pl.when(r != me)
        def _():
            remote(w_all.at[r], w_all.at[r], c_send.at[0], c_recv.at[r], 0).wait_recv()

        add_block(r)
        return carry

    lax.fori_loop(2, rows, later_block, 0)

    @pl.when(me == 0)
    def _():
        for c in range(CHUNKS):
            rest = jnp.zeros((step, block), F32)
            for s in range(rows - 2):
                p0_copy(c, s).wait_recv()
                rest = rest + got0[s, chunk(c)].astype(F32)
            tt_copy(c).wait_recv()
            rest = rest + got_t[chunk(c)].astype(F32)
            value = product(c_buf[chunk(c)] - rest, h1_buf[...], l1_buf[...])
            w_buf[chunk(c)] = value
            w_all[0, chunk(c)] = value.astype(BF16)
            for k in range(1, rows):
                w_copy(c, k).start()

    def w_wait(r):
        @pl.when(me != r)
        def _():
            for c in range(CHUNKS):
                remote(
                    w_all.at[r, chunk(c)],
                    w_all.at[r, chunk(c)],
                    w_send.at[c, 0],
                    w_recv.at[r, c],
                    0,
                ).wait_recv()

    w_wait(1)

    add_block(1)
    w_wait(0)

    add_block(0)

    for k in range(1, rows):
        t_copy(k).wait_send()

    @pl.when(me >= 2)
    def _():
        for c in range(CHUNKS):
            p1_copy(c, me - 2).wait_send()
            p0_copy(c, me - 2).wait_send()
        for k in range(1, rows):
            c_copy(k).wait_send()

    @pl.when(me == 1)
    def _():
        for c in range(CHUNKS):
            tt_copy(c).wait_send()

    @pl.when(me < 2)
    def _():
        for c in range(CHUNKS):
            for k in range(1, rows):
                w_copy(c, k).wait_send()


def on_device(
    coefficients, factor_panel, block_inverse, train_inputs, query_points, inv_length, amplitude
):
    rows = lax.axis_size("rows")
    m, block = coefficients.shape
    params = train_inputs.shape[0]
    width = query_points.shape[1] // rows
    padded = -(-params // 16) * 16
    depth = -(-(6 * padded + 16) // 128) * 128
    anywhere = pl.BlockSpec(memory_space=pltpu.HBM)
    dma = pltpu.SemaphoreType.DMA
    vmem = pltpu.VMEM
    solved, summed = pl.pallas_call(
        functools.partial(kernel, rows),
        out_shape=(
            pltpu.VMEM((m, block), F32),
            pltpu.VMEM((m, width), F32),
        ),
        in_specs=[pl.BlockSpec(memory_space=pltpu.SMEM)] + [anywhere] * 5,
        out_specs=(pl.BlockSpec(memory_space=pltpu.VMEM),) * 2,
        scratch_shapes=[
            vmem((m, block), F32),
            vmem((block, block), F32),
            vmem((block, block), F32),
            vmem((block, block), F32),
            vmem((params, width), F32),
            vmem((rows, params, block), F32),
            vmem((block, block), BF16),
            vmem((block, block), BF16),
            vmem((block, block), BF16),
            vmem((block, block), BF16),
            vmem((m, block), SEND_TYPE),
            vmem((m, block), SEND_TYPE),
            vmem((rows - 2, m, block), SEND_TYPE),
            vmem((rows - 2, m, block), SEND_TYPE),
            vmem((m, block), SEND_TYPE),
            vmem((rows, m, block), BF16),
            vmem((block, depth), BF16),
            vmem((depth, width), BF16),
            vmem((rows, block, width), BF16),
            dma((6,)),
            dma((rows - 1,)),
            dma((rows,)),
            dma((CHUNKS,)),
            dma((rows - 2, CHUNKS)),
            dma((CHUNKS,)),
            dma((rows - 2, CHUNKS)),
            dma((CHUNKS,)),
            dma((CHUNKS,)),
            dma((rows - 1,)),
            dma((rows,)),
            dma((CHUNKS, rows - 1)),
            dma((2, CHUNKS)),
        ],
        compiler_params=pltpu.CompilerParams(
            collective_id=0, has_side_effects=True, vmem_limit_bytes=60 * 1024 * 1024
        ),
    )(inv_length, coefficients, factor_panel, block_inverse, train_inputs, query_points)
    weights = jnp.where(lax.axis_index("rows") < 2, solved, coefficients)
    return (weights, summed * amplitude[:, None])


def solution(mesh):
    return jax.shard_map(
        on_device,
        mesh=mesh,
        in_specs=(
            P("cols", "rows"),
            P("rows", None),
            P("rows", None),
            P(None, "rows"),
            P(),
            P(),
            P("cols"),
        ),
        out_specs=(P("cols", "rows"), P("cols", "rows")),
        check_vma=False,
    )
```

```python
import functools

import jax
import jax.numpy as jnp
from jax import lax
from jax.experimental import pallas as pl
from jax.experimental.pallas import tpu as pltpu
from jax.sharding import PartitionSpec as P

CHUNKS = 4
EPSILON = 1e-06
BF16 = jnp.bfloat16
F32 = jnp.float32
SEND_TYPE = jnp.bfloat16


def split_two(x):
    high = x.astype(BF16)
    return high, (x - high.astype(F32)).astype(BF16)


def split_three(x):
    first = x.astype(BF16).astype(F32)
    rest = x - first
    second = rest.astype(BF16).astype(F32)
    third = (rest - second).astype(BF16).astype(F32)
    return first, second, third


def product(x, high, low):
    x_high, x_low = split_two(x)
    rows = x.shape[0]
    both = jnp.dot(
        jnp.concatenate([x_high, x_low], axis=0), high, preferred_element_type=F32
    )
    return both[:rows] + (both[rows:] + jnp.dot(x_high, low, preferred_element_type=F32))


def scaled_points(points, scale):
    params, count = points.shape
    padded = -(-params // 16) * 16
    x = (points - 0.5) * scale[:params]
    return jnp.concatenate([x, jnp.zeros((padded - params, count), F32)], axis=0)


def norm_rows(x, ones_first, added):
    count = x.shape[1]
    n1, n2, n3 = split_three(jnp.sum(x * x, axis=0, keepdims=True) + added)
    row = lax.broadcasted_iota(jnp.int32, (16, count), 0)
    at = 3 if ones_first else 0
    one_at = 0 if ones_first else 3
    out = jnp.where((row >= one_at) & (row < one_at + 3), 1.0, 0.0)
    out = jnp.where(row == at, n1, out)
    out = jnp.where(row == at + 1, n2, out)
    return jnp.where(row == at + 2, n3, out)


def kernel(
    rows,
    inv_ref,
    c_hbm,
    f_hbm,
    b_hbm,
    t_hbm,
    q_hbm,
    w_buf,
    acc,
    c_buf,
    f1_buf,
    f0_buf,
    b_buf,
    q_buf,
    t_all,
    h1_buf,
    l1_buf,
    h2_buf,
    l2_buf,
    part1,
    part0,
    got1,
    got0,
    got_t,
    w_all,
    a_t,
    q_aug,
    k_all,
    local_sem,
    t_send,
    t_recv,
    p1_send,
    p1_recv,
    p0_send,
    p0_recv,
    tt_send,
    tt_recv,
    c_send,
    c_recv,
    w_send,
    w_recv,
):
    me = lax.axis_index("rows")
    m, block = c_buf.shape
    params, width = q_buf.shape
    step = m // CHUNKS
    tile = 512 if width % 512 == 0 else width
    tiles = width // tile

    def load(src, dst, at):
        copy = pltpu.make_async_copy(src, dst, local_sem.at[at])
        copy.start()
        return copy

    def remote(src, dst, send, recv, peer):
        return pltpu.make_async_remote_copy(
            src_ref=src,
            dst_ref=dst,
            send_sem=send,
            recv_sem=recv,
            device_id={"rows": peer},
            device_id_type=pl.DeviceIdType.MESH,
        )

    in_c = load(c_hbm, c_buf, 0)
    in_f1 = load(f_hbm.at[:, pl.ds(block, block)], f1_buf, 1)
    in_t = load(t_hbm, t_all.at[me], 2)
    in_q = load(q_hbm.at[:, pl.ds(pl.multiple_of(me * width, 128), width)], q_buf, 3)
    in_f0 = load(f_hbm.at[:, pl.ds(0, block)], f0_buf, 4)
    in_b = load(b_hbm, b_buf, 5)

    barrier = pltpu.get_barrier_semaphore()
    for k in range(1, rows):
        pl.semaphore_signal(
            barrier,
            inc=1,
            device_id={"rows": lax.rem(me + k, rows)},
            device_id_type=pl.DeviceIdType.MESH,
        )
    pl.semaphore_wait(barrier, rows - 1)

    def t_copy(k):
        return remote(
            t_hbm, t_all.at[me], t_send.at[k - 1], t_recv.at[me], lax.rem(me + k, rows)
        )

    for k in range(1, rows):
        t_copy(k).start()

    def chunk(c):
        return pl.ds(c * step, step)

    def part(r):
        return pl.ds(pl.multiple_of(r * block, block), block)

    def p1_copy(c, slot):
        return remote(
            part1.at[chunk(c)],
            got1.at[slot, chunk(c)],
            p1_send.at[c],
            p1_recv.at[slot, c],
            1,
        )

    def p0_copy(c, slot):
        return remote(
            part0.at[chunk(c)],
            got0.at[slot, chunk(c)],
            p0_send.at[c],
            p0_recv.at[slot, c],
            0,
        )

    def tt_copy(c):
        return remote(
            part0.at[chunk(c)], got_t.at[chunk(c)], tt_send.at[c], tt_recv.at[c], 0
        )

    def c_copy(k):
        return remote(
            w_all.at[:, part(me)],
            w_all.at[:, part(me)],
            c_send.at[k - 1],
            c_recv.at[me],
            lax.rem(me + k, rows),
        )

    def w_copy(c, k):
        return remote(
            w_all.at[chunk(c), part(me)],
            w_all.at[chunk(c), part(me)],
            w_send.at[c, k - 1],
            w_recv.at[me, c],
            lax.rem(me + k, rows),
        )

    in_c.wait()
    in_f1.wait()

    @pl.when(me >= 2)
    def _():
        h1_buf[...], l1_buf[...] = split_two(f1_buf[...])
        for half in range(2):
            at = pl.ds(half * m // 2, m // 2)
            part1[at] = product(c_buf[at], h1_buf[...], l1_buf[...]).astype(SEND_TYPE)
            for c in range(half * CHUNKS // 2, (half + 1) * CHUNKS // 2):
                p1_copy(c, me - 2).start()
        w_all[:, part(me)] = c_buf[...].astype(BF16)

    in_f0.wait()
    in_b.wait()
    h2_buf[...], l2_buf[...] = split_two(f0_buf[...])

    @pl.when(me >= 2)
    def _():
        part0[...] = product(c_buf[...], h2_buf[...], l2_buf[...]).astype(SEND_TYPE)
        for c in range(CHUNKS):
            p0_copy(c, me - 2).start()

    @pl.when(me < 2)
    def _():
        h1_buf[...], l1_buf[...] = split_two(b_buf[...])

    row = lax.broadcasted_iota(jnp.int32, (params, 1), 0)
    scale = jnp.zeros((params, 1), F32)
    for d in range(params):
        scale = jnp.where(row == d, inv_ref[d], scale)
    in_q.wait()
    x = scaled_points(q_buf[...], scale)
    x1, x2, x3 = split_three(-2.0 * x)
    pieces = [x1, x2, x1, x3, x2, x1, norm_rows(x, True, EPSILON)]
    used = sum(piece.shape[0] for piece in pieces)
    depth = q_aug.shape[0]
    if depth > used:
        pieces.append(jnp.zeros((depth - used, width), F32))
    q_aug[...] = jnp.concatenate(pieces, axis=0).astype(BF16)

    def train_side(r):
        @pl.when(r == me)
        def _():
            in_t.wait()

        @pl.when(r != me)
        def _():
            remote(t_hbm, t_all.at[r], t_send.at[0], t_recv.at[r], 0).wait_recv()

        y = scaled_points(t_all[r], scale)
        y1, y2, y3 = split_three(y)
        parts = [y1, y1, y2, y1, y2, y3, norm_rows(y, False, 0.0)]
        if depth > used:
            parts.append(jnp.zeros((depth - used, block), F32))
        a_t[...] = jnp.concatenate(parts, axis=0).T.astype(BF16)

    def kernel_tile(j):
        at = pl.ds(pl.multiple_of(j * tile, 128), tile)
        y = jnp.dot(a_t[...], q_aug[:, at], preferred_element_type=F32)
        y = jnp.maximum(y, EPSILON)
        return at, jnp.exp(-(y * lax.rsqrt(y))).astype(BF16)

    def kernel_block(r, carry):
        train_side(r)

        def store_tile(j, inner):
            at, values = kernel_tile(j)
            k_all[part(r), at] = values
            return inner

        return lax.fori_loop(0, tiles, store_tile, carry)

    lax.fori_loop(0, 2, kernel_block, 0)

    @pl.when(me >= 2)
    def _():
        for k in range(1, rows):
            c_copy(k).start()

    @pl.when(me == 1)
    def _():
        for c in range(CHUNKS):
            rest = jnp.zeros((step, block), F32)
            for s in range(rows - 2):
                p1_copy(c, s).wait_recv()
                rest = rest + got1[s, chunk(c)].astype(F32)
            value = product(c_buf[chunk(c)] - rest, h1_buf[...], l1_buf[...])
            w_buf[chunk(c)] = value
            part0[chunk(c)] = product(value, h2_buf[...], l2_buf[...]).astype(SEND_TYPE)
            tt_copy(c).start()
            w_all[chunk(c), part(1)] = value.astype(BF16)
        for c in range(CHUNKS):
            for k in range(1, rows):
                w_copy(c, k).start()

    lax.fori_loop(2, rows, kernel_block, 0)

    @pl.when(me == 0)
    def _():
        for c in range(CHUNKS):
            rest = jnp.zeros((step, block), F32)
            for s in range(rows - 2):
                p0_copy(c, s).wait_recv()
                rest = rest + got0[s, chunk(c)].astype(F32)
            tt_copy(c).wait_recv()
            rest = rest + got_t[chunk(c)].astype(F32)
            value = product(c_buf[chunk(c)] - rest, h1_buf[...], l1_buf[...])
            w_buf[chunk(c)] = value
            w_all[chunk(c), part(0)] = value.astype(BF16)
            for k in range(1, rows):
                w_copy(c, k).start()

    def w_wait(r):
        @pl.when(me != r)
        def _():
            for c in range(CHUNKS):
                remote(
                    w_all.at[chunk(c), part(r)],
                    w_all.at[chunk(c), part(r)],
                    w_send.at[c, 0],
                    w_recv.at[r, c],
                    0,
                ).wait_recv()

    def later_block(r, carry):
        @pl.when(r != me)
        def _():
            remote(
                w_all.at[:, part(r)], w_all.at[:, part(r)], c_send.at[0], c_recv.at[r], 0
            ).wait_recv()

        return carry

    lax.fori_loop(2, rows, later_block, 0)
    w_wait(1)

    def first_tile(j, carry):
        at = pl.ds(pl.multiple_of(j * tile, 128), tile)
        acc[:, at] = jnp.dot(
            w_all[:, block:], k_all[block:, at], preferred_element_type=F32
        )
        return carry

    lax.fori_loop(0, tiles, first_tile, 0)
    w_wait(0)

    def last_tile(j, carry):
        at = pl.ds(pl.multiple_of(j * tile, 128), tile)
        acc[:, at] += jnp.dot(
            w_all[:, :block], k_all[:block, at], preferred_element_type=F32
        )
        return carry

    lax.fori_loop(0, tiles, last_tile, 0)

    for k in range(1, rows):
        t_copy(k).wait_send()

    @pl.when(me >= 2)
    def _():
        for c in range(CHUNKS):
            p1_copy(c, me - 2).wait_send()
            p0_copy(c, me - 2).wait_send()
        for k in range(1, rows):
            c_copy(k).wait_send()

    @pl.when(me == 1)
    def _():
        for c in range(CHUNKS):
            tt_copy(c).wait_send()

    @pl.when(me < 2)
    def _():
        for c in range(CHUNKS):
            for k in range(1, rows):
                w_copy(c, k).wait_send()


def on_device(
    coefficients, factor_panel, block_inverse, train_inputs, query_points, inv_length, amplitude
):
    rows = lax.axis_size("rows")
    m, block = coefficients.shape
    params = train_inputs.shape[0]
    width = query_points.shape[1] // rows
    padded = -(-params // 16) * 16
    depth = -(-(6 * padded + 16) // 128) * 128
    anywhere = pl.BlockSpec(memory_space=pltpu.HBM)
    dma = pltpu.SemaphoreType.DMA
    vmem = pltpu.VMEM
    solved, summed = pl.pallas_call(
        functools.partial(kernel, rows),
        out_shape=(
            pltpu.VMEM((m, block), F32),
            pltpu.VMEM((m, width), F32),
        ),
        in_specs=[pl.BlockSpec(memory_space=pltpu.SMEM)] + [anywhere] * 5,
        out_specs=(pl.BlockSpec(memory_space=pltpu.VMEM),) * 2,
        scratch_shapes=[
            vmem((m, block), F32),
            vmem((block, block), F32),
            vmem((block, block), F32),
            vmem((block, block), F32),
            vmem((params, width), F32),
            vmem((rows, params, block), F32),
            vmem((block, block), BF16),
            vmem((block, block), BF16),
            vmem((block, block), BF16),
            vmem((block, block), BF16),
            vmem((m, block), SEND_TYPE),
            vmem((m, block), SEND_TYPE),
            vmem((rows - 2, m, block), SEND_TYPE),
            vmem((rows - 2, m, block), SEND_TYPE),
            vmem((m, block), SEND_TYPE),
            vmem((m, rows * block), BF16),
            vmem((block, depth), BF16),
            vmem((depth, width), BF16),
            vmem((rows * block, width), BF16),
            dma((6,)),
            dma((rows - 1,)),
            dma((rows,)),
            dma((CHUNKS,)),
            dma((rows - 2, CHUNKS)),
            dma((CHUNKS,)),
            dma((rows - 2, CHUNKS)),
            dma((CHUNKS,)),
            dma((CHUNKS,)),
            dma((rows - 1,)),
            dma((rows,)),
            dma((CHUNKS, rows - 1)),
            dma((2, CHUNKS)),
        ],
        compiler_params=pltpu.CompilerParams(
            collective_id=0, has_side_effects=True, vmem_limit_bytes=60 * 1024 * 1024
        ),
    )(inv_length, coefficients, factor_panel, block_inverse, train_inputs, query_points)
    weights = jnp.where(lax.axis_index("rows") < 2, solved, coefficients)
    return (weights, summed * amplitude[:, None])


def solution(mesh):
    return jax.shard_map(
        on_device,
        mesh=mesh,
        in_specs=(
            P("cols", "rows"),
            P("rows", None),
            P("rows", None),
            P(None, "rows"),
            P(),
            P(),
            P("cols"),
        ),
        out_specs=(P("cols", "rows"), P("cols", "rows")),
        check_vma=False,
    )
```

```python
import functools

import jax
import jax.numpy as jnp
from jax import lax
from jax.experimental import pallas as pl
from jax.experimental.pallas import tpu as pltpu
from jax.sharding import PartitionSpec as P

CHUNKS = 4
EPSILON = 1e-06
BF16 = jnp.bfloat16
F32 = jnp.float32
SEND_TYPE = jnp.bfloat16


def split_two(x):
    high = x.astype(BF16)
    return high, (x - high.astype(F32)).astype(BF16)


def split_three(x):
    first = x.astype(BF16).astype(F32)
    rest = x - first
    second = rest.astype(BF16).astype(F32)
    third = (rest - second).astype(BF16).astype(F32)
    return first, second, third


def product(x, high, low):
    x_high, x_low = split_two(x)
    rows = x.shape[0]
    both = jnp.dot(
        jnp.concatenate([x_high, x_low], axis=0), high, preferred_element_type=F32
    )
    return both[:rows] + (both[rows:] + jnp.dot(x_high, low, preferred_element_type=F32))


def scaled_points(points, scale):
    params, count = points.shape
    padded = -(-params // 16) * 16
    x = (points - 0.5) * scale[:params]
    return jnp.concatenate([x, jnp.zeros((padded - params, count), F32)], axis=0)


def norm_rows(x, ones_first, added):
    count = x.shape[1]
    n1, n2, n3 = split_three(jnp.sum(x * x, axis=0, keepdims=True) + added)
    row = lax.broadcasted_iota(jnp.int32, (16, count), 0)
    at = 3 if ones_first else 0
    one_at = 0 if ones_first else 3
    out = jnp.where((row >= one_at) & (row < one_at + 3), 1.0, 0.0)
    out = jnp.where(row == at, n1, out)
    out = jnp.where(row == at + 1, n2, out)
    return jnp.where(row == at + 2, n3, out)


def kernel(
    rows,
    inv_ref,
    c_hbm,
    f_hbm,
    b_hbm,
    t_hbm,
    q_hbm,
    w_buf,
    p_out,
    c_buf,
    f1_buf,
    f0_buf,
    b_buf,
    q_buf,
    t_all,
    h1_buf,
    l1_buf,
    h2_buf,
    l2_buf,
    part1,
    part0,
    got1,
    got0,
    got_t,
    w_all,
    a_t,
    q_aug,
    k_all,
    acc,
    local_sem,
    t_send,
    t_recv,
    p1_send,
    p1_recv,
    p0_send,
    p0_recv,
    tt_send,
    tt_recv,
    c_send,
    c_recv,
    w_send,
    w_recv,
    nb_send,
    nb_recv,
    nc_send,
    nc_recv,
    r_send,
    r_recv,
):
    me = lax.axis_index("rows")
    m, block = c_buf.shape
    params, width = q_buf.shape
    step = m // CHUNKS
    tile = 512 if width % 512 == 0 else width
    tiles = width // tile
    column = lax.axis_index("cols")
    core = lax.rem(column, 2)
    partner = column + 1 - 2 * core

    def load(src, dst, at):
        copy = pltpu.make_async_copy(src, dst, local_sem.at[at])
        copy.start()
        return copy

    def near(src, dst, send, recv):
        return pltpu.make_async_remote_copy(
            src_ref=src,
            dst_ref=dst,
            send_sem=send,
            recv_sem=recv,
            device_id={"cols": partner},
            device_id_type=pl.DeviceIdType.MESH,
        )

    def remote(src, dst, send, recv, peer):
        return pltpu.make_async_remote_copy(
            src_ref=src,
            dst_ref=dst,
            send_sem=send,
            recv_sem=recv,
            device_id={"rows": peer},
            device_id_type=pl.DeviceIdType.MESH,
        )

    in_c = load(c_hbm, c_buf, 0)
    in_f1 = load(f_hbm.at[:, pl.ds(block, block)], f1_buf, 1)
    in_t = load(t_hbm, t_all.at[me], 2)
    in_q = load(q_hbm.at[:, pl.ds(pl.multiple_of((2 * me + core) * width, 128), width)], q_buf, 3)
    in_f0 = load(f_hbm.at[:, pl.ds(0, block)], f0_buf, 4)
    in_b = load(b_hbm, b_buf, 5)

    barrier = pltpu.get_barrier_semaphore()
    for k in range(1, rows):
        pl.semaphore_signal(
            barrier,
            inc=1,
            device_id={"rows": lax.rem(me + k, rows)},
            device_id_type=pl.DeviceIdType.MESH,
        )
    pl.semaphore_signal(
        barrier, inc=1, device_id={"cols": partner}, device_id_type=pl.DeviceIdType.MESH
    )
    pl.semaphore_wait(barrier, rows)

    def t_copy(k):
        return remote(
            t_hbm, t_all.at[me], t_send.at[k - 1], t_recv.at[me], lax.rem(me + k, rows)
        )

    for k in range(1, rows):
        t_copy(k).start()

    def chunk(c):
        return pl.ds(c * step, step)

    def part(r):
        return pl.ds(pl.multiple_of(r * block, block), block)

    def p1_copy(c, slot):
        return remote(
            part1.at[chunk(c)],
            got1.at[slot, chunk(c)],
            p1_send.at[c],
            p1_recv.at[slot, c],
            1,
        )

    def p0_copy(c, slot):
        return remote(
            part0.at[chunk(c)],
            got0.at[slot, chunk(c)],
            p0_send.at[c],
            p0_recv.at[slot, c],
            0,
        )

    def tt_copy(c):
        return remote(
            part0.at[chunk(c)], got_t.at[chunk(c)], tt_send.at[c], tt_recv.at[c], 0
        )

    def c_copy(k):
        return remote(
            w_all.at[pl.ds(0, m), part(me)],
            w_all.at[pl.ds(0, m), part(me)],
            c_send.at[k - 1],
            c_recv.at[me],
            lax.rem(me + k, rows),
        )

    def w_copy(c, k):
        return remote(
            w_all.at[chunk(c), part(me)],
            w_all.at[chunk(c), part(me)],
            w_send.at[c, k - 1],
            w_recv.at[me, c],
            lax.rem(me + k, rows),
        )

    def near_block(r):
        return near(
            w_all.at[pl.ds(0, m), part(r)],
            w_all.at[pl.ds(m, m), part(r)],
            nb_send.at[r],
            nb_recv.at[r],
        )

    def near_chunk(r, c):
        return near(
            w_all.at[chunk(c), part(r)],
            w_all.at[pl.ds(m + c * step, step), part(r)],
            nc_send.at[r, c],
            nc_recv.at[r, c],
        )

    others = [rows - 1] + list(range(1, rows - 1))

    in_c.wait()
    in_f1.wait()

    @pl.when(me >= 2)
    def _():
        h1_buf[...], l1_buf[...] = split_two(f1_buf[...])
        for half in range(2):
            at = pl.ds(half * m // 2, m // 2)
            part1[at] = product(c_buf[at], h1_buf[...], l1_buf[...]).astype(SEND_TYPE)
            for c in range(half * CHUNKS // 2, (half + 1) * CHUNKS // 2):
                p1_copy(c, me - 2).start()
        w_all[:m, part(me)] = c_buf[...].astype(BF16)

    in_f0.wait()
    in_b.wait()
    h2_buf[...], l2_buf[...] = split_two(f0_buf[...])

    @pl.when(me >= 2)
    def _():
        part0[...] = product(c_buf[...], h2_buf[...], l2_buf[...]).astype(SEND_TYPE)
        for c in range(CHUNKS):
            p0_copy(c, me - 2).start()

    @pl.when(me < 2)
    def _():
        h1_buf[...], l1_buf[...] = split_two(b_buf[...])

    row = lax.broadcasted_iota(jnp.int32, (params, 1), 0)
    scale = jnp.zeros((params, 1), F32)
    for d in range(params):
        scale = jnp.where(row == d, inv_ref[d], scale)
    in_q.wait()
    x = scaled_points(q_buf[...], scale)
    x1, x2, x3 = split_three(-2.0 * x)
    pieces = [x1, x2, x1, x3, x2, x1, norm_rows(x, True, EPSILON)]
    used = sum(piece.shape[0] for piece in pieces)
    depth = q_aug.shape[0]
    if depth > used:
        pieces.append(jnp.zeros((depth - used, width), F32))
    q_aug[...] = jnp.concatenate(pieces, axis=0).astype(BF16)

    def train_side(r):
        @pl.when(r == me)
        def _():
            in_t.wait()

        @pl.when(r != me)
        def _():
            remote(t_hbm, t_all.at[r], t_send.at[0], t_recv.at[r], 0).wait_recv()

        y = scaled_points(t_all[r], scale)
        y1, y2, y3 = split_three(y)
        parts = [y1, y1, y2, y1, y2, y3, norm_rows(y, False, 0.0)]
        if depth > used:
            parts.append(jnp.zeros((depth - used, block), F32))
        a_t[...] = jnp.concatenate(parts, axis=0).T.astype(BF16)

    def kernel_tile(j):
        at = pl.ds(pl.multiple_of(j * tile, 128), tile)
        y = jnp.dot(a_t[...], q_aug[:, at], preferred_element_type=F32)
        y = jnp.maximum(y, EPSILON)
        return at, jnp.exp(-(y * lax.rsqrt(y))).astype(BF16)

    def kernel_block(r, carry):
        train_side(r)

        def store_tile(j, inner):
            at, values = kernel_tile(j)
            k_all[part(r), at] = values
            return inner

        return lax.fori_loop(0, tiles, store_tile, carry)

    lax.fori_loop(0, 2, kernel_block, 0)

    @pl.when(me == 1)
    def _():
        for c in range(CHUNKS):
            rest = jnp.zeros((step, block), F32)
            for s in range(rows - 2):
                p1_copy(c, s).wait_recv()
                rest = rest + got1[s, chunk(c)].astype(F32)
            value = product(c_buf[chunk(c)] - rest, h1_buf[...], l1_buf[...])
            w_buf[chunk(c)] = value
            part0[chunk(c)] = product(value, h2_buf[...], l2_buf[...]).astype(SEND_TYPE)
            tt_copy(c).start()
            w_all[chunk(c), part(1)] = value.astype(BF16)
        for c in range(CHUNKS):
            for k in others:
                w_copy(c, k).start()
            near_chunk(1, c).start()

    lax.fori_loop(2, 3, kernel_block, 0)

    @pl.when(me >= 2)
    def _():
        for c in range(CHUNKS):
            p1_copy(c, me - 2).wait_send()
        for k in range(1, rows):
            c_copy(k).start()
        near_block(me).start()

    lax.fori_loop(3, rows, kernel_block, 0)

    @pl.when(me == 0)
    def _():
        for c in range(CHUNKS):
            rest = jnp.zeros((step, block), F32)
            for s in range(rows - 2):
                p0_copy(c, s).wait_recv()
                rest = rest + got0[s, chunk(c)].astype(F32)
            tt_copy(c).wait_recv()
            rest = rest + got_t[chunk(c)].astype(F32)
            value = product(c_buf[chunk(c)] - rest, h1_buf[...], l1_buf[...])
            w_buf[chunk(c)] = value
            w_all[chunk(c), part(0)] = value.astype(BF16)
            for k in others:
                w_copy(c, k).start()
            near_chunk(0, c).start()

    def pass_on(r):
        @pl.when(me != r)
        def _():
            for c in range(CHUNKS):
                remote(
                    w_all.at[chunk(c), part(r)],
                    w_all.at[chunk(c), part(r)],
                    w_send.at[c, 0],
                    w_recv.at[r, c],
                    0,
                ).wait_recv()
                near_chunk(r, c).start()

        for c in range(CHUNKS):
            near_chunk(r, c).wait_recv()

    def pass_block(r, carry):
        @pl.when(r != me)
        def _():
            remote(
                w_all.at[pl.ds(0, m), part(r)],
                w_all.at[pl.ds(0, m), part(r)],
                c_send.at[0],
                c_recv.at[r],
                0,
            ).wait_recv()
            near_block(r).start()

        return carry

    def block_arrived(r, carry):
        near_block(r).wait_recv()
        return carry

    lax.fori_loop(2, rows, pass_block, 0)
    lax.fori_loop(2, rows, block_arrived, 0)

    def later_tile(j, carry):
        at = pl.ds(pl.multiple_of(j * tile, 128), tile)
        acc[:, at] = jnp.dot(
            w_all[:, 2 * block :], k_all[2 * block :, at], preferred_element_type=F32
        )
        return carry

    lax.fori_loop(0, tiles, later_tile, 0)
    pass_on(1)

    def one_tile(j, carry):
        at = pl.ds(pl.multiple_of(j * tile, 128), tile)
        acc[:, at] += jnp.dot(
            w_all[:, block : 2 * block], k_all[block : 2 * block, at], preferred_element_type=F32
        )
        return carry

    lax.fori_loop(0, tiles, one_tile, 0)
    pass_on(0)

    def result_copy(j):
        at = pl.ds(j * tile, tile)
        out_at = pl.ds(pl.multiple_of(core * width + j * tile, 128), tile)
        return near(acc.at[pl.ds(m, m), at], p_out.at[:, out_at], r_send.at[j], r_recv.at[j])

    for j in range(tiles):
        at = pl.ds(j * tile, tile)
        value = acc[:, at] + jnp.dot(
            w_all[:, :block], k_all[:block, at], preferred_element_type=F32
        )
        acc[m:, at] = value[m:]
        result_copy(j).start()
        p_out[:, pl.ds(pl.multiple_of(core * width + j * tile, 128), tile)] = value[:m]

    for j in range(tiles):
        result_copy(j).wait()

    for r in range(2):
        for c in range(CHUNKS):
            near_chunk(r, c).wait_send()

    def block_sent(r, carry):
        near_block(r).wait_send()
        return carry

    lax.fori_loop(2, rows, block_sent, 0)

    for k in range(1, rows):
        t_copy(k).wait_send()

    @pl.when(me >= 2)
    def _():
        for c in range(CHUNKS):
            p0_copy(c, me - 2).wait_send()
        for k in range(1, rows):
            c_copy(k).wait_send()

    @pl.when(me == 1)
    def _():
        for c in range(CHUNKS):
            tt_copy(c).wait_send()

    @pl.when(me < 2)
    def _():
        for c in range(CHUNKS):
            for k in range(1, rows):
                w_copy(c, k).wait_send()


def on_device(
    coefficients, factor_panel, block_inverse, train_inputs, query_points, inv_length, amplitude
):
    rows = lax.axis_size("rows")
    m, block = coefficients.shape
    params = train_inputs.shape[0]
    width = query_points.shape[1] // (2 * rows)
    tile = 512 if width % 512 == 0 else width
    padded = -(-params // 16) * 16
    depth = -(-(6 * padded + 16) // 128) * 128
    anywhere = pl.BlockSpec(memory_space=pltpu.HBM)
    dma = pltpu.SemaphoreType.DMA
    vmem = pltpu.VMEM
    solved, summed = pl.pallas_call(
        functools.partial(kernel, rows),
        out_shape=(
            pltpu.VMEM((m, block), F32),
            pltpu.VMEM((m, 2 * width), F32),
        ),
        in_specs=[pl.BlockSpec(memory_space=pltpu.SMEM)] + [anywhere] * 5,
        out_specs=(pl.BlockSpec(memory_space=pltpu.VMEM),) * 2,
        scratch_shapes=[
            vmem((m, block), F32),
            vmem((block, block), F32),
            vmem((block, block), F32),
            vmem((block, block), F32),
            vmem((params, width), F32),
            vmem((rows, params, block), F32),
            vmem((block, block), BF16),
            vmem((block, block), BF16),
            vmem((block, block), BF16),
            vmem((block, block), BF16),
            vmem((m, block), SEND_TYPE),
            vmem((m, block), SEND_TYPE),
            vmem((rows - 2, m, block), SEND_TYPE),
            vmem((rows - 2, m, block), SEND_TYPE),
            vmem((m, block), SEND_TYPE),
            vmem((2 * m, rows * block), BF16),
            vmem((block, depth), BF16),
            vmem((depth, width), BF16),
            vmem((rows * block, width), BF16),
            vmem((2 * m, width), F32),
            dma((6,)),
            dma((rows - 1,)),
            dma((rows,)),
            dma((CHUNKS,)),
            dma((rows - 2, CHUNKS)),
            dma((CHUNKS,)),
            dma((rows - 2, CHUNKS)),
            dma((CHUNKS,)),
            dma((CHUNKS,)),
            dma((rows - 1,)),
            dma((rows,)),
            dma((CHUNKS, rows - 1)),
            dma((2, CHUNKS)),
            dma((rows,)),
            dma((rows,)),
            dma((2, CHUNKS)),
            dma((2, CHUNKS)),
            dma((width // tile,)),
            dma((width // tile,)),
        ],
        compiler_params=pltpu.CompilerParams(
            collective_id=0, has_side_effects=True, vmem_limit_bytes=60 * 1024 * 1024
        ),
    )(inv_length, coefficients, factor_panel, block_inverse, train_inputs, query_points)
    weights = jnp.where(lax.axis_index("rows") < 2, solved, coefficients)
    return (weights, summed * amplitude[:, None])


def solution(mesh):
    return jax.shard_map(
        on_device,
        mesh=mesh,
        in_specs=(
            P("cols", "rows"),
            P("rows", None),
            P("rows", None),
            P(None, "rows"),
            P(),
            P(),
            P("cols"),
        ),
        out_specs=(P("cols", "rows"), P("cols", "rows")),
        check_vma=False,
    )
```

```python
import functools

import jax
import jax.numpy as jnp
from jax import lax
from jax.experimental import pallas as pl
from jax.experimental.pallas import tpu as pltpu
from jax.sharding import PartitionSpec as P

CHUNKS = 4
EPSILON = 1e-06
BF16 = jnp.bfloat16
F32 = jnp.float32
SEND_TYPE = jnp.bfloat16


def split_two(x):
    high = x.astype(BF16)
    return high, (x - high.astype(F32)).astype(BF16)


def split_three(x):
    first = x.astype(BF16).astype(F32)
    rest = x - first
    second = rest.astype(BF16).astype(F32)
    third = (rest - second).astype(BF16).astype(F32)
    return first, second, third


def product(x, high, low):
    x_high, x_low = split_two(x)
    rows = x.shape[0]
    both = jnp.dot(
        jnp.concatenate([x_high, x_low], axis=0), high, preferred_element_type=F32
    )
    return both[:rows] + (both[rows:] + jnp.dot(x_high, low, preferred_element_type=F32))


def scaled_points(points, scale):
    params, count = points.shape
    padded = -(-params // 16) * 16
    x = (points - 0.5) * scale[:params]
    return jnp.concatenate([x, jnp.zeros((padded - params, count), F32)], axis=0)


def norm_rows(x, ones_first, added):
    count = x.shape[1]
    n1, n2, n3 = split_three(jnp.sum(x * x, axis=0, keepdims=True) + added)
    row = lax.broadcasted_iota(jnp.int32, (16, count), 0)
    at = 3 if ones_first else 0
    one_at = 0 if ones_first else 3
    out = jnp.where((row >= one_at) & (row < one_at + 3), 1.0, 0.0)
    out = jnp.where(row == at, n1, out)
    out = jnp.where(row == at + 1, n2, out)
    return jnp.where(row == at + 2, n3, out)


def kernel(
    rows,
    inv_ref,
    c_hbm,
    f_hbm,
    b_hbm,
    t_hbm,
    q_hbm,
    w_buf,
    acc,
    c_buf,
    f1_buf,
    f0_buf,
    b_buf,
    q_buf,
    t_all,
    h1_buf,
    l1_buf,
    h2_buf,
    l2_buf,
    part1,
    part0,
    got1,
    got0,
    got_t,
    w_all,
    a_t,
    q_aug,
    k_all,
    local_sem,
    t_send,
    t_recv,
    p1_send,
    p1_recv,
    p0_send,
    p0_recv,
    tt_send,
    tt_recv,
    c_send,
    c_recv,
    w_send,
    w_recv,
    relay_send,
    k_send,
    k_recv,
):
    me = lax.axis_index("rows")
    m, block = c_buf.shape
    params, width = q_buf.shape
    step = m // CHUNKS
    tile = 512 if width % 512 == 0 else width
    tiles = width // tile
    column = lax.axis_index("cols")
    core = lax.rem(column, 2)
    partner = column + 1 - 2 * core
    relayed = rows == 4

    def load(src, dst, at):
        copy = pltpu.make_async_copy(src, dst, local_sem.at[at])
        copy.start()
        return copy

    def remote(src, dst, send, recv, peer):
        return pltpu.make_async_remote_copy(
            src_ref=src,
            dst_ref=dst,
            send_sem=send,
            recv_sem=recv,
            device_id={"rows": peer},
            device_id_type=pl.DeviceIdType.MESH,
        )

    in_c = load(c_hbm, c_buf, 0)
    in_f1 = load(f_hbm.at[:, pl.ds(block, block)], f1_buf, 1)
    in_t = load(t_hbm, t_all.at[me], 2)
    in_q = load(q_hbm.at[:, pl.ds(pl.multiple_of((2 * me + core) * width, 128), width)], q_buf, 3)
    in_f0 = load(f_hbm.at[:, pl.ds(0, block)], f0_buf, 4)
    in_b = load(b_hbm, b_buf, 5)

    barrier = pltpu.get_barrier_semaphore()
    for k in range(1, rows):
        pl.semaphore_signal(
            barrier,
            inc=1,
            device_id={"rows": lax.rem(me + k, rows)},
            device_id_type=pl.DeviceIdType.MESH,
        )
    pl.semaphore_signal(
        barrier, inc=1, device_id={"cols": partner}, device_id_type=pl.DeviceIdType.MESH
    )
    pl.semaphore_wait(barrier, rows)

    def t_copy(k):
        return remote(
            t_hbm, t_all.at[me], t_send.at[k - 1], t_recv.at[me], lax.rem(me + k, rows)
        )

    for k in range(1, rows):
        t_copy(k).start()

    def chunk(c):
        return pl.ds(c * step, step)

    def part(r):
        return pl.ds(pl.multiple_of(r * block, block), block)

    def p1_copy(c, slot):
        return remote(
            part1.at[chunk(c)],
            got1.at[slot, chunk(c)],
            p1_send.at[c],
            p1_recv.at[slot, c],
            1,
        )

    def p0_copy(c, slot):
        return remote(
            part0.at[chunk(c)],
            got0.at[slot, chunk(c)],
            p0_send.at[c],
            p0_recv.at[slot, c],
            0,
        )

    def tt_copy(c):
        return remote(
            part0.at[chunk(c)], got_t.at[chunk(c)], tt_send.at[c], tt_recv.at[c], 0
        )

    def c_copy(k):
        return remote(
            w_all.at[:, part(me)],
            w_all.at[:, part(me)],
            c_send.at[k - 1],
            c_recv.at[me],
            lax.rem(me + k, rows),
        )

    def w_copy(c, k):
        return remote(
            w_all.at[chunk(c), part(me)],
            w_all.at[chunk(c), part(me)],
            w_send.at[c, k - 1],
            w_recv.at[me, c],
            lax.rem(me + k, rows),
        )

    def k_copy(r, j, half):
        at = pl.ds(pl.multiple_of(half * width + j * tile, 128), tile)
        return pltpu.make_async_remote_copy(
            src_ref=k_all.at[part(r), at],
            dst_ref=k_all.at[part(r), at],
            send_sem=k_send.at[r, j],
            recv_sem=k_recv.at[r, j],
            device_id={"cols": partner},
            device_id_type=pl.DeviceIdType.MESH,
        )

    def relay_copy(c, r, to):
        return remote(
            w_all.at[chunk(c), part(r)],
            w_all.at[chunk(c), part(r)],
            relay_send.at[c],
            w_recv.at[r, c],
            to,
        )

    from_one = [3, 2] if relayed else [rows - 1] + list(range(1, rows - 1))
    from_zero = [2, 1] if relayed else list(range(1, rows))

    in_c.wait()
    in_f1.wait()

    @pl.when(me >= 2)
    def _():
        h1_buf[...], l1_buf[...] = split_two(f1_buf[...])
        for half in range(2):
            at = pl.ds(half * m // 2, m // 2)
            part1[at] = product(c_buf[at], h1_buf[...], l1_buf[...]).astype(SEND_TYPE)
            for c in range(half * CHUNKS // 2, (half + 1) * CHUNKS // 2):
                p1_copy(c, me - 2).start()
        w_all[:, part(me)] = c_buf[...].astype(BF16)

    in_f0.wait()
    in_b.wait()
    h2_buf[...], l2_buf[...] = split_two(f0_buf[...])

    @pl.when(me >= 2)
    def _():
        part0[...] = product(c_buf[...], h2_buf[...], l2_buf[...]).astype(SEND_TYPE)
        for c in range(CHUNKS):
            p0_copy(c, me - 2).start()

    @pl.when(me < 2)
    def _():
        h1_buf[...], l1_buf[...] = split_two(b_buf[...])

    row = lax.broadcasted_iota(jnp.int32, (params, 1), 0)
    scale = jnp.zeros((params, 1), F32)
    for d in range(params):
        scale = jnp.where(row == d, inv_ref[d], scale)
    in_q.wait()
    x = scaled_points(q_buf[...], scale)
    x1, x2, x3 = split_three(-2.0 * x)
    pieces = [x1, x2, x1, x3, x2, x1, norm_rows(x, True, EPSILON)]
    used = sum(piece.shape[0] for piece in pieces)
    depth = q_aug.shape[0]
    if depth > used:
        pieces.append(jnp.zeros((depth - used, width), F32))
    q_aug[...] = jnp.concatenate(pieces, axis=0).astype(BF16)

    def train_side(r):
        @pl.when(r == me)
        def _():
            in_t.wait()

        @pl.when(r != me)
        def _():
            remote(t_hbm, t_all.at[r], t_send.at[0], t_recv.at[r], 0).wait_recv()

        y = scaled_points(t_all[r], scale)
        y1, y2, y3 = split_three(y)
        parts = [y1, y1, y2, y1, y2, y3, norm_rows(y, False, 0.0)]
        if depth > used:
            parts.append(jnp.zeros((depth - used, block), F32))
        a_t[...] = jnp.concatenate(parts, axis=0).T.astype(BF16)

    def kernel_block(n, carry):
        r = lax.rem(n + 2, rows)
        train_side(r)

        def store_tile(j, inner):
            here = pl.ds(pl.multiple_of(j * tile, 128), tile)
            at = pl.ds(pl.multiple_of(core * width + j * tile, 128), tile)
            y = jnp.dot(a_t[...], q_aug[:, here], preferred_element_type=F32)
            y = jnp.maximum(y, EPSILON)
            k_all[part(r), at] = jnp.exp(-(y * lax.rsqrt(y))).astype(BF16)
            k_copy(r, j, core).start()
            return inner

        return lax.fori_loop(0, tiles, store_tile, carry)

    lax.fori_loop(0, 2, kernel_block, 0)

    @pl.when(me == 1)
    def _():
        for c in range(CHUNKS):
            rest = jnp.zeros((step, block), F32)
            for s in range(rows - 2):
                p1_copy(c, s).wait_recv()
                rest = rest + got1[s, chunk(c)].astype(F32)
            value = product(c_buf[chunk(c)] - rest, h1_buf[...], l1_buf[...])
            w_buf[chunk(c)] = value
            part0[chunk(c)] = product(value, h2_buf[...], l2_buf[...]).astype(SEND_TYPE)
            tt_copy(c).start()
            w_all[chunk(c), part(1)] = value.astype(BF16)
        for c in range(CHUNKS):
            for k in from_one:
                w_copy(c, k).start()

    lax.fori_loop(2, 3, kernel_block, 0)

    @pl.when(me >= 2)
    def _():
        for c in range(CHUNKS):
            p1_copy(c, me - 2).wait_send()
        for k in range(1, rows):
            c_copy(k).start()

    lax.fori_loop(3, rows, kernel_block, 0)

    @pl.when(me == 0)
    def _():
        for c in range(CHUNKS):
            rest = jnp.zeros((step, block), F32)
            for s in range(rows - 2):
                p0_copy(c, s).wait_recv()
                rest = rest + got0[s, chunk(c)].astype(F32)
            tt_copy(c).wait_recv()
            rest = rest + got_t[chunk(c)].astype(F32)
            value = product(c_buf[chunk(c)] - rest, h1_buf[...], l1_buf[...])
            w_buf[chunk(c)] = value
            w_all[chunk(c), part(0)] = value.astype(BF16)
            for k in from_zero:
                w_copy(c, k).start()

    def w_wait(r):
        @pl.when(me != r)
        def _():
            for c in range(CHUNKS):
                relay_copy(c, r, 0).wait_recv()
                if relayed:

                    @pl.when(me == 2 + r)
                    def _():
                        relay_copy(c, r, 3 - r).start()

    def k_wait(r, carry):
        for j in range(tiles):
            k_copy(r, j, 1 - core).wait_recv()
        return carry

    def add_blocks(first, last, fresh):
        def add_tile(j, carry):
            at = pl.ds(pl.multiple_of(j * tile, 128), tile)
            value = jnp.dot(
                w_all[:, first * block : last * block],
                k_all[first * block : last * block, at],
                preferred_element_type=F32,
            )
            acc[:, at] = value if fresh else acc[:, at] + value
            return carry

        lax.fori_loop(0, 2 * tiles, add_tile, 0)

    def later_block(r, carry):
        @pl.when(r != me)
        def _():
            remote(
                w_all.at[:, part(r)], w_all.at[:, part(r)], c_send.at[0], c_recv.at[r], 0
            ).wait_recv()

        return k_wait(r, carry)

    lax.fori_loop(2, rows, later_block, 0)
    add_blocks(2, rows, True)
    w_wait(1)
    k_wait(1, 0)
    add_blocks(1, 2, False)
    k_wait(0, 0)
    w_wait(0)
    add_blocks(0, 1, False)

    def k_sent(r, carry):
        for j in range(tiles):
            k_copy(r, j, core).wait_send()
        return carry

    lax.fori_loop(0, rows, k_sent, 0)

    for k in range(1, rows):
        t_copy(k).wait_send()

    @pl.when(me >= 2)
    def _():
        for c in range(CHUNKS):
            p0_copy(c, me - 2).wait_send()
            if relayed:
                relay_copy(c, 0, 0).wait_send()
        for k in range(1, rows):
            c_copy(k).wait_send()

    @pl.when(me == 1)
    def _():
        for c in range(CHUNKS):
            tt_copy(c).wait_send()

    for r, peers in ((0, from_zero), (1, from_one)):

        @pl.when(me == r)
        def _():
            for c in range(CHUNKS):
                for k in peers:
                    w_copy(c, k).wait_send()


def on_device(
    coefficients, factor_panel, block_inverse, train_inputs, query_points, inv_length, amplitude
):
    rows = lax.axis_size("rows")
    m, block = coefficients.shape
    params = train_inputs.shape[0]
    width = query_points.shape[1] // (2 * rows)
    tile = 512 if width % 512 == 0 else width
    padded = -(-params // 16) * 16
    depth = -(-(6 * padded + 16) // 128) * 128
    anywhere = pl.BlockSpec(memory_space=pltpu.HBM)
    dma = pltpu.SemaphoreType.DMA
    vmem = pltpu.VMEM
    solved, summed = pl.pallas_call(
        functools.partial(kernel, rows),
        out_shape=(
            pltpu.VMEM((m, block), F32),
            pltpu.VMEM((m, 2 * width), F32),
        ),
        in_specs=[pl.BlockSpec(memory_space=pltpu.SMEM)] + [anywhere] * 5,
        out_specs=(pl.BlockSpec(memory_space=pltpu.VMEM),) * 2,
        scratch_shapes=[
            vmem((m, block), F32),
            vmem((block, block), F32),
            vmem((block, block), F32),
            vmem((block, block), F32),
            vmem((params, width), F32),
            vmem((rows, params, block), F32),
            vmem((block, block), BF16),
            vmem((block, block), BF16),
            vmem((block, block), BF16),
            vmem((block, block), BF16),
            vmem((m, block), SEND_TYPE),
            vmem((m, block), SEND_TYPE),
            vmem((rows - 2, m, block), SEND_TYPE),
            vmem((rows - 2, m, block), SEND_TYPE),
            vmem((m, block), SEND_TYPE),
            vmem((m, rows * block), BF16),
            vmem((block, depth), BF16),
            vmem((depth, width), BF16),
            vmem((rows * block, 2 * width), BF16),
            dma((6,)),
            dma((rows - 1,)),
            dma((rows,)),
            dma((CHUNKS,)),
            dma((rows - 2, CHUNKS)),
            dma((CHUNKS,)),
            dma((rows - 2, CHUNKS)),
            dma((CHUNKS,)),
            dma((CHUNKS,)),
            dma((rows - 1,)),
            dma((rows,)),
            dma((CHUNKS, rows - 1)),
            dma((2, CHUNKS)),
            dma((CHUNKS,)),
            dma((rows, width // tile)),
            dma((rows, width // tile)),
        ],
        compiler_params=pltpu.CompilerParams(
            collective_id=0, has_side_effects=True, vmem_limit_bytes=60 * 1024 * 1024
        ),
    )(inv_length, coefficients, factor_panel, block_inverse, train_inputs, query_points)
    weights = jnp.where(lax.axis_index("rows") < 2, solved, coefficients)
    return (weights, summed * amplitude[:, None])


def solution(mesh):
    return jax.shard_map(
        on_device,
        mesh=mesh,
        in_specs=(
            P("cols", "rows"),
            P("rows", None),
            P("rows", None),
            P(None, "rows"),
            P(),
            P(),
            P("cols"),
        ),
        out_specs=(P("cols", "rows"), P("cols", "rows")),
        check_vma=False,
    )
```

```python
import functools

import jax
import jax.numpy as jnp
from jax import lax
from jax.experimental import pallas as pl
from jax.experimental.pallas import tpu as pltpu
from jax.sharding import PartitionSpec as P

CHUNKS = 4
EPSILON = 1e-06
BF16 = jnp.bfloat16
F32 = jnp.float32
SEND_TYPE = jnp.bfloat16


def split_two(x):
    high = x.astype(BF16)
    return high, (x - high.astype(F32)).astype(BF16)


def split_three(x):
    first = x.astype(BF16).astype(F32)
    rest = x - first
    second = rest.astype(BF16).astype(F32)
    third = (rest - second).astype(BF16).astype(F32)
    return first, second, third


def product(x, high, low):
    x_high, x_low = split_two(x)
    rows = x.shape[0]
    both = jnp.dot(
        jnp.concatenate([x_high, x_low], axis=0), high, preferred_element_type=F32
    )
    return both[:rows] + (both[rows:] + jnp.dot(x_high, low, preferred_element_type=F32))


def scaled_points(points, scale):
    params, count = points.shape
    padded = -(-params // 16) * 16
    x = (points - 0.5) * scale[:params]
    return jnp.concatenate([x, jnp.zeros((padded - params, count), F32)], axis=0)


def norm_rows(x, ones_first, added):
    count = x.shape[1]
    n1, n2, n3 = split_three(jnp.sum(x * x, axis=0, keepdims=True) + added)
    row = lax.broadcasted_iota(jnp.int32, (16, count), 0)
    at = 3 if ones_first else 0
    one_at = 0 if ones_first else 3
    out = jnp.where((row >= one_at) & (row < one_at + 3), 1.0, 0.0)
    out = jnp.where(row == at, n1, out)
    out = jnp.where(row == at + 1, n2, out)
    return jnp.where(row == at + 2, n3, out)


def kernel(
    rows,
    inv_ref,
    c_hbm,
    f_hbm,
    b_hbm,
    t_hbm,
    q_hbm,
    w_buf,
    acc,
    c_buf,
    f1_buf,
    f0_buf,
    b_buf,
    q_buf,
    t_all,
    h1_buf,
    l1_buf,
    h2_buf,
    l2_buf,
    part1,
    part0,
    got1,
    got0,
    got_t,
    w_all,
    a_t,
    q_aug,
    k_all,
    local_sem,
    t_send,
    t_recv,
    p1_send,
    p1_recv,
    p0_send,
    p0_recv,
    tt_send,
    tt_recv,
    c_send,
    c_recv,
    w_send,
    w_recv,
    k_send,
    k_recv,
):
    me = lax.axis_index("rows")
    m, block = c_buf.shape
    params, width = q_buf.shape
    step = m // CHUNKS
    tile = 512 if width % 512 == 0 else width
    tiles = width // tile
    column = lax.axis_index("cols")
    core = lax.rem(column, 2)
    partner = column + 1 - 2 * core

    def load(src, dst, at):
        copy = pltpu.make_async_copy(src, dst, local_sem.at[at])
        copy.start()
        return copy

    def remote(src, dst, send, recv, peer):
        return pltpu.make_async_remote_copy(
            src_ref=src,
            dst_ref=dst,
            send_sem=send,
            recv_sem=recv,
            device_id={"rows": peer},
            device_id_type=pl.DeviceIdType.MESH,
        )

    in_c = load(c_hbm, c_buf, 0)
    in_f1 = load(f_hbm.at[:, pl.ds(block, block)], f1_buf, 1)
    in_t = load(t_hbm, t_all.at[me], 2)
    in_q = load(q_hbm.at[:, pl.ds(pl.multiple_of((2 * me + core) * width, 128), width)], q_buf, 3)
    in_f0 = load(f_hbm.at[:, pl.ds(0, block)], f0_buf, 4)
    in_b = load(b_hbm, b_buf, 5)

    barrier = pltpu.get_barrier_semaphore()
    for k in range(1, rows):
        pl.semaphore_signal(
            barrier,
            inc=1,
            device_id={"rows": lax.rem(me + k, rows)},
            device_id_type=pl.DeviceIdType.MESH,
        )
    pl.semaphore_signal(
        barrier, inc=1, device_id={"cols": partner}, device_id_type=pl.DeviceIdType.MESH
    )
    pl.semaphore_wait(barrier, rows)

    def t_copy(k):
        return remote(
            t_hbm, t_all.at[me], t_send.at[k - 1], t_recv.at[me], lax.rem(me + k, rows)
        )

    for k in range(1, rows):
        t_copy(k).start()

    def chunk(c):
        return pl.ds(c * step, step)

    def part(r):
        return pl.ds(pl.multiple_of(r * block, block), block)

    def p1_copy(c, slot):
        return remote(
            part1.at[chunk(c)],
            got1.at[slot, chunk(c)],
            p1_send.at[c],
            p1_recv.at[slot, c],
            1,
        )

    def p0_copy(c, slot):
        return remote(
            part0.at[chunk(c)],
            got0.at[slot, chunk(c)],
            p0_send.at[c],
            p0_recv.at[slot, c],
            0,
        )

    def tt_copy(c):
        return remote(
            part0.at[chunk(c)], got_t.at[chunk(c)], tt_send.at[c], tt_recv.at[c], 0
        )

    def c_copy(k):
        return remote(
            w_all.at[:, part(me)],
            w_all.at[:, part(me)],
            c_send.at[k - 1],
            c_recv.at[me],
            lax.rem(me + k, rows),
        )

    def w_copy(c, k):
        return remote(
            w_all.at[chunk(c), part(me)],
            w_all.at[chunk(c), part(me)],
            w_send.at[c, k - 1],
            w_recv.at[me, c],
            lax.rem(me + k, rows),
        )

    def k_copy(r, j, half):
        at = pl.ds(pl.multiple_of(half * width + j * tile, 128), tile)
        return pltpu.make_async_remote_copy(
            src_ref=k_all.at[part(r), at],
            dst_ref=k_all.at[part(r), at],
            send_sem=k_send.at[r, j],
            recv_sem=k_recv.at[r, j],
            device_id={"cols": partner},
            device_id_type=pl.DeviceIdType.MESH,
        )

    from_one = [rows - 1] + list(range(1, rows - 1))
    from_zero = list(range(rows - 1, 0, -1))

    in_c.wait()
    in_f1.wait()

    @pl.when(me >= 2)
    def _():
        h1_buf[...], l1_buf[...] = split_two(f1_buf[...])
        for half in range(2):
            at = pl.ds(half * m // 2, m // 2)
            part1[at] = product(c_buf[at], h1_buf[...], l1_buf[...]).astype(SEND_TYPE)
            for c in range(half * CHUNKS // 2, (half + 1) * CHUNKS // 2):
                p1_copy(c, me - 2).start()
        w_all[:, part(me)] = c_buf[...].astype(BF16)

    in_f0.wait()
    in_b.wait()
    h2_buf[...], l2_buf[...] = split_two(f0_buf[...])

    @pl.when(me >= 2)
    def _():
        part0[...] = product(c_buf[...], h2_buf[...], l2_buf[...]).astype(SEND_TYPE)
        for c in range(CHUNKS):
            p0_copy(c, me - 2).start()

    @pl.when(me < 2)
    def _():
        h1_buf[...], l1_buf[...] = split_two(b_buf[...])

    row = lax.broadcasted_iota(jnp.int32, (params, 1), 0)
    scale = jnp.zeros((params, 1), F32)
    for d in range(params):
        scale = jnp.where(row == d, inv_ref[d], scale)
    in_q.wait()
    x = scaled_points(q_buf[...], scale)
    x1, x2, x3 = split_three(-2.0 * x)
    pieces = [x1, x2, x1, x3, x2, x1, norm_rows(x, True, EPSILON)]
    used = sum(piece.shape[0] for piece in pieces)
    depth = q_aug.shape[0]
    if depth > used:
        pieces.append(jnp.zeros((depth - used, width), F32))
    q_aug[...] = jnp.concatenate(pieces, axis=0).astype(BF16)

    def train_side(r):
        @pl.when(r == me)
        def _():
            in_t.wait()

        @pl.when(r != me)
        def _():
            remote(t_hbm, t_all.at[r], t_send.at[0], t_recv.at[r], 0).wait_recv()

        y = scaled_points(t_all[r], scale)
        y1, y2, y3 = split_three(y)
        parts = [y1, y1, y2, y1, y2, y3, norm_rows(y, False, 0.0)]
        if depth > used:
            parts.append(jnp.zeros((depth - used, block), F32))
        a_t[...] = jnp.concatenate(parts, axis=0).T.astype(BF16)

    def kernel_block(n, carry):
        r = lax.rem(n + 2, rows)
        train_side(r)

        def store_tile(j, inner):
            here = pl.ds(pl.multiple_of(j * tile, 128), tile)
            at = pl.ds(pl.multiple_of(core * width + j * tile, 128), tile)
            y = jnp.dot(a_t[...], q_aug[:, here], preferred_element_type=F32)
            y = jnp.maximum(y, EPSILON)
            k_all[part(r), at] = jnp.exp(-(y * lax.rsqrt(y))).astype(BF16)
            k_copy(r, j, core).start()
            return inner

        return lax.fori_loop(0, tiles, store_tile, carry)

    lax.fori_loop(0, 2, kernel_block, 0)

    @pl.when(me == 1)
    def _():
        for c in range(CHUNKS):
            rest = jnp.zeros((step, block), F32)
            for s in range(rows - 2):
                p1_copy(c, s).wait_recv()
                rest = rest + got1[s, chunk(c)].astype(F32)
            value = product(c_buf[chunk(c)] - rest, h1_buf[...], l1_buf[...])
            w_buf[chunk(c)] = value
            part0[chunk(c)] = product(value, h2_buf[...], l2_buf[...]).astype(SEND_TYPE)
            tt_copy(c).start()
            w_all[chunk(c), part(1)] = value.astype(BF16)
        for c in range(CHUNKS):
            for k in from_one:
                w_copy(c, k).start()

    lax.fori_loop(2, 3, kernel_block, 0)

    @pl.when(me >= 2)
    def _():
        for c in range(CHUNKS):
            p1_copy(c, me - 2).wait_send()
        for k in range(1, rows):
            c_copy(k).start()

    lax.fori_loop(3, rows, kernel_block, 0)

    @pl.when(me == 0)
    def _():
        for c in range(CHUNKS):
            rest = jnp.zeros((step, block), F32)
            for s in range(rows - 2):
                p0_copy(c, s).wait_recv()
                rest = rest + got0[s, chunk(c)].astype(F32)
            tt_copy(c).wait_recv()
            rest = rest + got_t[chunk(c)].astype(F32)
            value = product(c_buf[chunk(c)] - rest, h1_buf[...], l1_buf[...])
            w_buf[chunk(c)] = value
            w_all[chunk(c), part(0)] = value.astype(BF16)
            for k in from_zero:
                w_copy(c, k).start()

    def w_wait(r):
        @pl.when(me != r)
        def _():
            for c in range(CHUNKS):
                remote(
                    w_all.at[chunk(c), part(r)],
                    w_all.at[chunk(c), part(r)],
                    w_send.at[c, 0],
                    w_recv.at[r, c],
                    0,
                ).wait_recv()

    def k_wait(r, carry):
        for j in range(tiles):
            k_copy(r, j, 1 - core).wait_recv()
        return carry

    def add_blocks(first, last, fresh):
        def add_tile(j, carry):
            at = pl.ds(pl.multiple_of(j * tile, 128), tile)
            value = jnp.dot(
                w_all[:, first * block : last * block],
                k_all[first * block : last * block, at],
                preferred_element_type=F32,
            )
            acc[:, at] = value if fresh else acc[:, at] + value
            return carry

        lax.fori_loop(0, 2 * tiles, add_tile, 0)

    def later_block(r, carry):
        @pl.when(r != me)
        def _():
            remote(
                w_all.at[:, part(r)], w_all.at[:, part(r)], c_send.at[0], c_recv.at[r], 0
            ).wait_recv()

        return k_wait(r, carry)

    lax.fori_loop(2, rows, later_block, 0)
    add_blocks(2, rows, True)
    w_wait(1)
    k_wait(1, 0)
    add_blocks(1, 2, False)
    k_wait(0, 0)
    w_wait(0)
    add_blocks(0, 1, False)

    def k_sent(r, carry):
        for j in range(tiles):
            k_copy(r, j, core).wait_send()
        return carry

    lax.fori_loop(0, rows, k_sent, 0)

    for k in range(1, rows):
        t_copy(k).wait_send()

    @pl.when(me >= 2)
    def _():
        for c in range(CHUNKS):
            p0_copy(c, me - 2).wait_send()
        for k in range(1, rows):
            c_copy(k).wait_send()

    @pl.when(me == 1)
    def _():
        for c in range(CHUNKS):
            tt_copy(c).wait_send()

    for r, peers in ((0, from_zero), (1, from_one)):

        @pl.when(me == r)
        def _():
            for c in range(CHUNKS):
                for k in peers:
                    w_copy(c, k).wait_send()


def on_device(
    coefficients, factor_panel, block_inverse, train_inputs, query_points, inv_length, amplitude
):
    rows = lax.axis_size("rows")
    m, block = coefficients.shape
    params = train_inputs.shape[0]
    width = query_points.shape[1] // (2 * rows)
    tile = 512 if width % 512 == 0 else width
    padded = -(-params // 16) * 16
    depth = -(-(6 * padded + 16) // 128) * 128
    anywhere = pl.BlockSpec(memory_space=pltpu.HBM)
    dma = pltpu.SemaphoreType.DMA
    vmem = pltpu.VMEM
    solved, summed = pl.pallas_call(
        functools.partial(kernel, rows),
        out_shape=(
            pltpu.VMEM((m, block), F32),
            pltpu.VMEM((m, 2 * width), F32),
        ),
        in_specs=[pl.BlockSpec(memory_space=pltpu.SMEM)] + [anywhere] * 5,
        out_specs=(pl.BlockSpec(memory_space=pltpu.VMEM),) * 2,
        scratch_shapes=[
            vmem((m, block), F32),
            vmem((block, block), F32),
            vmem((block, block), F32),
            vmem((block, block), F32),
            vmem((params, width), F32),
            vmem((rows, params, block), F32),
            vmem((block, block), BF16),
            vmem((block, block), BF16),
            vmem((block, block), BF16),
            vmem((block, block), BF16),
            vmem((m, block), SEND_TYPE),
            vmem((m, block), SEND_TYPE),
            vmem((rows - 2, m, block), SEND_TYPE),
            vmem((rows - 2, m, block), SEND_TYPE),
            vmem((m, block), SEND_TYPE),
            vmem((m, rows * block), BF16),
            vmem((block, depth), BF16),
            vmem((depth, width), BF16),
            vmem((rows * block, 2 * width), BF16),
            dma((6,)),
            dma((rows - 1,)),
            dma((rows,)),
            dma((CHUNKS,)),
            dma((rows - 2, CHUNKS)),
            dma((CHUNKS,)),
            dma((rows - 2, CHUNKS)),
            dma((CHUNKS,)),
            dma((CHUNKS,)),
            dma((rows - 1,)),
            dma((rows,)),
            dma((CHUNKS, rows - 1)),
            dma((2, CHUNKS)),
            dma((rows, width // tile)),
            dma((rows, width // tile)),
        ],
        compiler_params=pltpu.CompilerParams(
            collective_id=0, has_side_effects=True, vmem_limit_bytes=60 * 1024 * 1024
        ),
    )(inv_length, coefficients, factor_panel, block_inverse, train_inputs, query_points)
    weights = jnp.where(lax.axis_index("rows") < 2, solved, coefficients)
    return (weights, summed * amplitude[:, None])


def solution(mesh):
    return jax.shard_map(
        on_device,
        mesh=mesh,
        in_specs=(
            P("cols", "rows"),
            P("rows", None),
            P("rows", None),
            P(None, "rows"),
            P(),
            P(),
            P("cols"),
        ),
        out_specs=(P("cols", "rows"), P("cols", "rows")),
        check_vma=False,
    )
```

```python
import functools

import jax
import jax.numpy as jnp
from jax import lax
from jax.experimental import pallas as pl
from jax.experimental.pallas import tpu as pltpu
from jax.sharding import PartitionSpec as P

CHUNKS = 4
EPSILON = 1e-06
BF16 = jnp.bfloat16
F32 = jnp.float32
SEND_TYPE = jnp.bfloat16


def split_two(x):
    high = x.astype(BF16)
    return high, (x - high.astype(F32)).astype(BF16)


def split_three(x):
    first = x.astype(BF16).astype(F32)
    rest = x - first
    second = rest.astype(BF16).astype(F32)
    third = (rest - second).astype(BF16).astype(F32)
    return first, second, third


def product(x, high, low):
    x_high, x_low = split_two(x)
    rows = x.shape[0]
    both = jnp.dot(
        jnp.concatenate([x_high, x_low], axis=0), high, preferred_element_type=F32
    )
    return both[:rows] + (both[rows:] + jnp.dot(x_high, low, preferred_element_type=F32))


def scaled_points(points, scale):
    params, count = points.shape
    padded = -(-params // 16) * 16
    x = (points - 0.5) * scale[:params]
    return jnp.concatenate([x, jnp.zeros((padded - params, count), F32)], axis=0)


def norm_rows(x, ones_first, added):
    count = x.shape[1]
    n1, n2, n3 = split_three(jnp.sum(x * x, axis=0, keepdims=True) + added)
    row = lax.broadcasted_iota(jnp.int32, (16, count), 0)
    at = 3 if ones_first else 0
    one_at = 0 if ones_first else 3
    out = jnp.where((row >= one_at) & (row < one_at + 3), 1.0, 0.0)
    out = jnp.where(row == at, n1, out)
    out = jnp.where(row == at + 1, n2, out)
    return jnp.where(row == at + 2, n3, out)


def kernel(
    rows,
    inv_ref,
    c_hbm,
    f_hbm,
    b_hbm,
    t_hbm,
    q_hbm,
    w_buf,
    acc,
    c_buf,
    f1_buf,
    f0_buf,
    b_buf,
    q_buf,
    t_all,
    h1_buf,
    l1_buf,
    h2_buf,
    l2_buf,
    part1,
    part0,
    got1,
    got0,
    got_t,
    w_all,
    a_t,
    q_aug,
    k_all,
    local_sem,
    t_send,
    t_recv,
    p1_send,
    p1_recv,
    p0_send,
    p0_recv,
    tt_send,
    tt_recv,
    c_send,
    c_recv,
    w_send,
    w_recv,
    relay_send,
    k_send,
    k_recv,
):
    me = lax.axis_index("rows")
    m, block = c_buf.shape
    params, width = q_buf.shape
    step = m // CHUNKS
    tile = 512 if width % 512 == 0 else width
    tiles = width // tile
    column = lax.axis_index("cols")
    core = lax.rem(column, 2)
    partner = column + 1 - 2 * core

    def load(src, dst, at):
        copy = pltpu.make_async_copy(src, dst, local_sem.at[at])
        copy.start()
        return copy

    def remote(src, dst, send, recv, peer):
        return pltpu.make_async_remote_copy(
            src_ref=src,
            dst_ref=dst,
            send_sem=send,
            recv_sem=recv,
            device_id={"rows": peer},
            device_id_type=pl.DeviceIdType.MESH,
        )

    in_c = load(c_hbm, c_buf, 0)
    in_f1 = load(f_hbm.at[:, pl.ds(block, block)], f1_buf, 1)
    in_t = load(t_hbm, t_all.at[me], 2)
    in_q = load(q_hbm.at[:, pl.ds(pl.multiple_of((2 * me + core) * width, 128), width)], q_buf, 3)
    in_f0 = load(f_hbm.at[:, pl.ds(0, block)], f0_buf, 4)
    in_b = load(b_hbm, b_buf, 5)

    barrier = pltpu.get_barrier_semaphore()
    for k in range(1, rows):
        pl.semaphore_signal(
            barrier,
            inc=1,
            device_id={"rows": lax.rem(me + k, rows)},
            device_id_type=pl.DeviceIdType.MESH,
        )
    pl.semaphore_signal(
        barrier, inc=1, device_id={"cols": partner}, device_id_type=pl.DeviceIdType.MESH
    )
    pl.semaphore_wait(barrier, rows)

    def t_copy(k):
        return remote(
            t_hbm, t_all.at[me], t_send.at[k - 1], t_recv.at[me], lax.rem(me + k, rows)
        )

    for k in range(1, rows):
        t_copy(k).start()

    def chunk(c):
        return pl.ds(c * step, step)

    def part(r):
        return pl.ds(pl.multiple_of(r * block, block), block)

    def p1_copy(c, slot):
        return remote(
            part1.at[chunk(c)],
            got1.at[slot, chunk(c)],
            p1_send.at[c],
            p1_recv.at[slot, c],
            1,
        )

    def p0_copy(c, slot):
        return remote(
            part0.at[chunk(c)],
            got0.at[slot, chunk(c)],
            p0_send.at[c],
            p0_recv.at[slot, c],
            0,
        )

    def tt_copy(c):
        return remote(
            part0.at[chunk(c)], got_t.at[chunk(c)], tt_send.at[c], tt_recv.at[c], 0
        )

    def c_copy(k):
        return remote(
            w_all.at[:, part(me)],
            w_all.at[:, part(me)],
            c_send.at[k - 1],
            c_recv.at[me],
            lax.rem(me + k, rows),
        )

    def w_copy(c, k):
        return remote(
            w_all.at[chunk(c), part(me)],
            w_all.at[chunk(c), part(me)],
            w_send.at[c, k - 1],
            w_recv.at[me, c],
            lax.rem(me + k, rows),
        )

    def k_copy(r, j, half):
        at = pl.ds(pl.multiple_of(half * width + j * tile, 128), tile)
        return pltpu.make_async_remote_copy(
            src_ref=k_all.at[part(r), at],
            dst_ref=k_all.at[part(r), at],
            send_sem=k_send.at[r, j],
            recv_sem=k_recv.at[r, j],
            device_id={"cols": partner},
            device_id_type=pl.DeviceIdType.MESH,
        )

    relayed = rows == 4
    from_one = [rows - 1, 2] if relayed else [rows - 1] + list(range(1, rows - 1))
    from_zero = list(range(rows - 1, 0, -1))

    in_c.wait()
    in_f1.wait()

    @pl.when(me >= 2)
    def _():
        h1_buf[...], l1_buf[...] = split_two(f1_buf[...])
        for half in range(2):
            at = pl.ds(half * m // 2, m // 2)
            part1[at] = product(c_buf[at], h1_buf[...], l1_buf[...]).astype(SEND_TYPE)
            for c in range(half * CHUNKS // 2, (half + 1) * CHUNKS // 2):
                p1_copy(c, me - 2).start()
        w_all[:, part(me)] = c_buf[...].astype(BF16)

    in_f0.wait()
    in_b.wait()
    h2_buf[...], l2_buf[...] = split_two(f0_buf[...])

    @pl.when(me >= 2)
    def _():
        part0[...] = product(c_buf[...], h2_buf[...], l2_buf[...]).astype(SEND_TYPE)
        for c in range(CHUNKS):
            p0_copy(c, me - 2).start()

    @pl.when(me < 2)
    def _():
        h1_buf[...], l1_buf[...] = split_two(b_buf[...])

    row = lax.broadcasted_iota(jnp.int32, (params, 1), 0)
    scale = jnp.zeros((params, 1), F32)
    for d in range(params):
        scale = jnp.where(row == d, inv_ref[d], scale)
    in_q.wait()
    x = scaled_points(q_buf[...], scale)
    x1, x2, x3 = split_three(-2.0 * x)
    pieces = [x1, x2, x1, x3, x2, x1, norm_rows(x, True, EPSILON)]
    used = sum(piece.shape[0] for piece in pieces)
    depth = q_aug.shape[0]
    if depth > used:
        pieces.append(jnp.zeros((depth - used, width), F32))
    q_aug[...] = jnp.concatenate(pieces, axis=0).astype(BF16)

    def train_side(r):
        @pl.when(r == me)
        def _():
            in_t.wait()

        @pl.when(r != me)
        def _():
            remote(t_hbm, t_all.at[r], t_send.at[0], t_recv.at[r], 0).wait_recv()

        y = scaled_points(t_all[r], scale)
        y1, y2, y3 = split_three(y)
        parts = [y1, y1, y2, y1, y2, y3, norm_rows(y, False, 0.0)]
        if depth > used:
            parts.append(jnp.zeros((depth - used, block), F32))
        a_t[...] = jnp.concatenate(parts, axis=0).T.astype(BF16)

    def kernel_block(n, carry):
        r = lax.rem(n + 2, rows)
        train_side(r)

        def store_tile(j, inner):
            here = pl.ds(pl.multiple_of(j * tile, 128), tile)
            at = pl.ds(pl.multiple_of(core * width + j * tile, 128), tile)
            y = jnp.dot(a_t[...], q_aug[:, here], preferred_element_type=F32)
            y = jnp.maximum(y, EPSILON)
            k_all[part(r), at] = jnp.exp(-(y * lax.rsqrt(y))).astype(BF16)
            k_copy(r, j, core).start()
            return inner

        return lax.fori_loop(0, tiles, store_tile, carry)

    lax.fori_loop(0, 2, kernel_block, 0)

    @pl.when(me == 1)
    def _():
        for c in range(CHUNKS):
            rest = jnp.zeros((step, block), F32)
            for s in range(rows - 2):
                p1_copy(c, s).wait_recv()
                rest = rest + got1[s, chunk(c)].astype(F32)
            value = product(c_buf[chunk(c)] - rest, h1_buf[...], l1_buf[...])
            w_buf[chunk(c)] = value
            part0[chunk(c)] = product(value, h2_buf[...], l2_buf[...]).astype(SEND_TYPE)
            tt_copy(c).start()
            w_all[chunk(c), part(1)] = value.astype(BF16)
        for c in range(CHUNKS):
            for k in from_one:
                w_copy(c, k).start()

    lax.fori_loop(2, 3, kernel_block, 0)

    @pl.when(me >= 2)
    def _():
        for c in range(CHUNKS):
            p1_copy(c, me - 2).wait_send()
        for k in range(1, rows):
            c_copy(k).start()

    lax.fori_loop(3, rows, kernel_block, 0)

    @pl.when(me == 0)
    def _():
        for c in range(CHUNKS):
            rest = jnp.zeros((step, block), F32)
            for s in range(rows - 2):
                p0_copy(c, s).wait_recv()
                rest = rest + got0[s, chunk(c)].astype(F32)
            tt_copy(c).wait_recv()
            rest = rest + got_t[chunk(c)].astype(F32)
            value = product(c_buf[chunk(c)] - rest, h1_buf[...], l1_buf[...])
            w_buf[chunk(c)] = value
            w_all[chunk(c), part(0)] = value.astype(BF16)
            for k in from_zero:
                w_copy(c, k).start()

    def w_arrival(c, r):
        return remote(
            w_all.at[chunk(c), part(r)],
            w_all.at[chunk(c), part(r)],
            relay_send.at[c],
            w_recv.at[r, c],
            2,
        )

    if relayed:

        @pl.when(me == 3)
        def _():
            for c in range(CHUNKS):
                w_arrival(c, 1).wait_recv()
                w_arrival(c, 1).start()

    def w_wait(r):
        @pl.when((me != 1) & (me != 3) if relayed and r == 1 else me != r)
        def _():
            for c in range(CHUNKS):
                w_arrival(c, r).wait_recv()

    def k_wait(r, carry):
        for j in range(tiles):
            k_copy(r, j, 1 - core).wait_recv()
        return carry

    def add_blocks(first, last, fresh):
        def add_tile(j, carry):
            at = pl.ds(pl.multiple_of(j * tile, 128), tile)
            value = jnp.dot(
                w_all[:, first * block : last * block],
                k_all[first * block : last * block, at],
                preferred_element_type=F32,
            )
            acc[:, at] = value if fresh else acc[:, at] + value
            return carry

        lax.fori_loop(0, 2 * tiles, add_tile, 0)

    def later_block(r, carry):
        @pl.when(r != me)
        def _():
            remote(
                w_all.at[:, part(r)], w_all.at[:, part(r)], c_send.at[0], c_recv.at[r], 0
            ).wait_recv()

        return k_wait(r, carry)

    lax.fori_loop(2, rows, later_block, 0)
    add_blocks(2, rows, True)
    w_wait(1)
    k_wait(1, 0)
    add_blocks(1, 2, False)
    k_wait(0, 0)
    w_wait(0)
    add_blocks(0, 1, False)

    def k_sent(r, carry):
        for j in range(tiles):
            k_copy(r, j, core).wait_send()
        return carry

    lax.fori_loop(0, rows, k_sent, 0)

    for k in range(1, rows):
        t_copy(k).wait_send()

    @pl.when(me >= 2)
    def _():
        for c in range(CHUNKS):
            p0_copy(c, me - 2).wait_send()
        for k in range(1, rows):
            c_copy(k).wait_send()

    @pl.when(me == 1)
    def _():
        for c in range(CHUNKS):
            tt_copy(c).wait_send()

    if relayed:

        @pl.when(me == 3)
        def _():
            for c in range(CHUNKS):
                w_arrival(c, 1).wait_send()

    for r, peers in ((0, from_zero), (1, from_one)):

        @pl.when(me == r)
        def _():
            for c in range(CHUNKS):
                for k in peers:
                    w_copy(c, k).wait_send()


def on_device(
    coefficients, factor_panel, block_inverse, train_inputs, query_points, inv_length, amplitude
):
    rows = lax.axis_size("rows")
    m, block = coefficients.shape
    params = train_inputs.shape[0]
    width = query_points.shape[1] // (2 * rows)
    tile = 512 if width % 512 == 0 else width
    padded = -(-params // 16) * 16
    depth = -(-(6 * padded + 16) // 128) * 128
    anywhere = pl.BlockSpec(memory_space=pltpu.HBM)
    dma = pltpu.SemaphoreType.DMA
    vmem = pltpu.VMEM
    solved, summed = pl.pallas_call(
        functools.partial(kernel, rows),
        out_shape=(
            pltpu.VMEM((m, block), F32),
            pltpu.VMEM((m, 2 * width), F32),
        ),
        in_specs=[pl.BlockSpec(memory_space=pltpu.SMEM)] + [anywhere] * 5,
        out_specs=(pl.BlockSpec(memory_space=pltpu.VMEM),) * 2,
        scratch_shapes=[
            vmem((m, block), F32),
            vmem((block, block), F32),
            vmem((block, block), F32),
            vmem((block, block), F32),
            vmem((params, width), F32),
            vmem((rows, params, block), F32),
            vmem((block, block), BF16),
            vmem((block, block), BF16),
            vmem((block, block), BF16),
            vmem((block, block), BF16),
            vmem((m, block), SEND_TYPE),
            vmem((m, block), SEND_TYPE),
            vmem((rows - 2, m, block), SEND_TYPE),
            vmem((rows - 2, m, block), SEND_TYPE),
            vmem((m, block), SEND_TYPE),
            vmem((m, rows * block), BF16),
            vmem((block, depth), BF16),
            vmem((depth, width), BF16),
            vmem((rows * block, 2 * width), BF16),
            dma((6,)),
            dma((rows - 1,)),
            dma((rows,)),
            dma((CHUNKS,)),
            dma((rows - 2, CHUNKS)),
            dma((CHUNKS,)),
            dma((rows - 2, CHUNKS)),
            dma((CHUNKS,)),
            dma((CHUNKS,)),
            dma((rows - 1,)),
            dma((rows,)),
            dma((CHUNKS, rows - 1)),
            dma((2, CHUNKS)),
            dma((CHUNKS,)),
            dma((rows, width // tile)),
            dma((rows, width // tile)),
        ],
        compiler_params=pltpu.CompilerParams(
            collective_id=0, has_side_effects=True, vmem_limit_bytes=60 * 1024 * 1024
        ),
    )(inv_length, coefficients, factor_panel, block_inverse, train_inputs, query_points)
    weights = jnp.where(lax.axis_index("rows") < 2, solved, coefficients)
    return (weights, summed * amplitude[:, None])


def solution(mesh):
    return jax.shard_map(
        on_device,
        mesh=mesh,
        in_specs=(
            P("cols", "rows"),
            P("rows", None),
            P("rows", None),
            P(None, "rows"),
            P(),
            P(),
            P("cols"),
        ),
        out_specs=(P("cols", "rows"), P("cols", "rows")),
        check_vma=False,
    )
```

```python
import functools

import jax
import jax.numpy as jnp
from jax import lax
from jax.experimental import pallas as pl
from jax.experimental.pallas import tpu as pltpu
from jax.sharding import PartitionSpec as P

CHUNKS = 4
EPSILON = 1e-06
BF16 = jnp.bfloat16
F32 = jnp.float32
SEND_TYPE = jnp.bfloat16


def split_two(x):
    high = x.astype(BF16)
    return high, (x - high.astype(F32)).astype(BF16)


def split_three(x):
    first = x.astype(BF16).astype(F32)
    rest = x - first
    second = rest.astype(BF16).astype(F32)
    third = (rest - second).astype(BF16).astype(F32)
    return first, second, third


def product(x, high, low):
    x_high, x_low = split_two(x)
    rows = x.shape[0]
    both = jnp.dot(
        jnp.concatenate([x_high, x_low], axis=0), high, preferred_element_type=F32
    )
    return both[:rows] + (both[rows:] + jnp.dot(x_high, low, preferred_element_type=F32))


def scaled_points(points, scale):
    params, count = points.shape
    padded = -(-params // 16) * 16
    x = (points - 0.5) * scale[:params]
    return jnp.concatenate([x, jnp.zeros((padded - params, count), F32)], axis=0)


def norm_rows(x, ones_first, added):
    count = x.shape[1]
    n1, n2, n3 = split_three(jnp.sum(x * x, axis=0, keepdims=True) + added)
    row = lax.broadcasted_iota(jnp.int32, (16, count), 0)
    at = 3 if ones_first else 0
    one_at = 0 if ones_first else 3
    out = jnp.where((row >= one_at) & (row < one_at + 3), 1.0, 0.0)
    out = jnp.where(row == at, n1, out)
    out = jnp.where(row == at + 1, n2, out)
    return jnp.where(row == at + 2, n3, out)


def kernel(
    rows,
    inv_ref,
    c_hbm,
    f_hbm,
    b_hbm,
    t_hbm,
    q_hbm,
    w_buf,
    acc,
    c_buf,
    f1_buf,
    f0_buf,
    b_buf,
    q_buf,
    t_all,
    h1_buf,
    l1_buf,
    h2_buf,
    l2_buf,
    part1,
    part0,
    got1,
    got0,
    got_t,
    w_all,
    a_t,
    q_aug,
    k_all,
    local_sem,
    t_send,
    t_recv,
    p1_send,
    p1_recv,
    p0_send,
    p0_recv,
    tt_send,
    tt_recv,
    c_send,
    c_recv,
    w_send,
    w_recv,
    k_send,
    k_recv,
):
    me = lax.axis_index("rows")
    m, block = c_buf.shape
    params, width = q_buf.shape
    step = m // CHUNKS
    tile = 512 if width % 512 == 0 else width
    tiles = width // tile
    column = lax.axis_index("cols")
    core = lax.rem(column, 2)
    partner = column + 1 - 2 * core

    def load(src, dst, at):
        copy = pltpu.make_async_copy(src, dst, local_sem.at[at])
        copy.start()
        return copy

    def remote(src, dst, send, recv, peer):
        return pltpu.make_async_remote_copy(
            src_ref=src,
            dst_ref=dst,
            send_sem=send,
            recv_sem=recv,
            device_id={"rows": peer},
            device_id_type=pl.DeviceIdType.MESH,
        )

    in_c = load(c_hbm, c_buf, 0)
    in_f1 = load(f_hbm.at[:, pl.ds(block, block)], f1_buf, 1)
    in_t = load(t_hbm, t_all.at[me], 2)
    in_q = load(q_hbm.at[:, pl.ds(pl.multiple_of((2 * me + core) * width, 128), width)], q_buf, 3)
    in_f0 = load(f_hbm.at[:, pl.ds(0, block)], f0_buf, 4)
    in_b = load(b_hbm, b_buf, 5)

    barrier = pltpu.get_barrier_semaphore()
    for k in range(1, rows):
        pl.semaphore_signal(
            barrier,
            inc=1,
            device_id={"rows": lax.rem(me + k, rows)},
            device_id_type=pl.DeviceIdType.MESH,
        )
    pl.semaphore_signal(
        barrier, inc=1, device_id={"cols": partner}, device_id_type=pl.DeviceIdType.MESH
    )
    pl.semaphore_wait(barrier, rows)

    def t_copy(k):
        return remote(
            t_hbm, t_all.at[me], t_send.at[k - 1], t_recv.at[me], lax.rem(me + k, rows)
        )

    for k in range(1, rows):
        t_copy(k).start()

    def chunk(c):
        return pl.ds(c * step, step)

    def part(r):
        return pl.ds(pl.multiple_of(r * block, block), block)

    def p1_copy(c, slot):
        return remote(
            part1.at[chunk(c)],
            got1.at[slot, chunk(c)],
            p1_send.at[c],
            p1_recv.at[slot, c],
            1,
        )

    def p0_copy(c, slot):
        return remote(
            part0.at[chunk(c)],
            got0.at[slot, chunk(c)],
            p0_send.at[c],
            p0_recv.at[slot, c],
            0,
        )

    def tt_copy(c):
        return remote(
            part0.at[chunk(c)], got_t.at[chunk(c)], tt_send.at[c], tt_recv.at[c], 0
        )

    def c_copy(k):
        return remote(
            w_all.at[:, part(me)],
            w_all.at[:, part(me)],
            c_send.at[k - 1],
            c_recv.at[me],
            lax.rem(me + k, rows),
        )

    def w_copy(c, k):
        return remote(
            w_all.at[chunk(c), part(me)],
            w_all.at[chunk(c), part(me)],
            w_send.at[c, k - 1],
            w_recv.at[me, c],
            lax.rem(me + k, rows),
        )

    def k_copy(r, j, half):
        at = pl.ds(pl.multiple_of(half * width + j * tile, 128), tile)
        return pltpu.make_async_remote_copy(
            src_ref=k_all.at[part(r), at],
            dst_ref=k_all.at[part(r), at],
            send_sem=k_send.at[r, j],
            recv_sem=k_recv.at[r, j],
            device_id={"cols": partner},
            device_id_type=pl.DeviceIdType.MESH,
        )

    from_one = [rows - 1] + list(range(1, rows - 1))
    from_zero = list(range(rows - 1, 0, -1))

    in_c.wait()
    in_f1.wait()

    @pl.when(me >= 2)
    def _():
        h1_buf[...], l1_buf[...] = split_two(f1_buf[...])
        for half in range(2):
            at = pl.ds(half * m // 2, m // 2)
            part1[at] = product(c_buf[at], h1_buf[...], l1_buf[...]).astype(SEND_TYPE)
            for c in range(half * CHUNKS // 2, (half + 1) * CHUNKS // 2):
                p1_copy(c, me - 2).start()
        w_all[:, part(me)] = c_buf[...].astype(BF16)

    in_f0.wait()
    in_b.wait()
    h2_buf[...], l2_buf[...] = split_two(f0_buf[...])

    @pl.when(me >= 2)
    def _():
        part0[...] = product(c_buf[...], h2_buf[...], l2_buf[...]).astype(SEND_TYPE)
        for c in range(CHUNKS):
            p0_copy(c, me - 2).start()

    @pl.when(me < 2)
    def _():
        h1_buf[...], l1_buf[...] = split_two(b_buf[...])

    row = lax.broadcasted_iota(jnp.int32, (params, 1), 0)
    scale = jnp.zeros((params, 1), F32)
    for d in range(params):
        scale = jnp.where(row == d, inv_ref[d], scale)
    in_q.wait()
    x = scaled_points(q_buf[...], scale)
    x1, x2, x3 = split_three(-2.0 * x)
    pieces = [x1, x2, x1, x3, x2, x1, norm_rows(x, True, EPSILON)]
    used = sum(piece.shape[0] for piece in pieces)
    depth = q_aug.shape[0]
    if depth > used:
        pieces.append(jnp.zeros((depth - used, width), F32))
    q_aug[...] = jnp.concatenate(pieces, axis=0).astype(BF16)

    def train_side(r):
        @pl.when(r == me)
        def _():
            in_t.wait()

        @pl.when(r != me)
        def _():
            remote(t_hbm, t_all.at[r], t_send.at[0], t_recv.at[r], 0).wait_recv()

        y = scaled_points(t_all[r], scale)
        y1, y2, y3 = split_three(y)
        parts = [y1, y1, y2, y1, y2, y3, norm_rows(y, False, 0.0)]
        if depth > used:
            parts.append(jnp.zeros((depth - used, block), F32))
        a_t[...] = jnp.concatenate(parts, axis=0).T.astype(BF16)

    def kernel_block(n, carry):
        r = lax.rem(n + 2, rows)
        train_side(r)

        def store_tile(j, inner):
            here = pl.ds(pl.multiple_of(j * tile, 128), tile)
            at = pl.ds(pl.multiple_of(core * width + j * tile, 128), tile)
            y = jnp.dot(a_t[...], q_aug[:, here], preferred_element_type=F32)
            y = jnp.maximum(y, EPSILON)
            k_all[part(r), at] = jnp.exp(-(y * lax.rsqrt(y))).astype(BF16)
            k_copy(r, j, core).start()
            return inner

        return lax.fori_loop(0, tiles, store_tile, carry)

    lax.fori_loop(0, 2, kernel_block, 0)

    @pl.when(me >= 2)
    def _():
        for k in range(1, rows):
            c_copy(k).start()

    @pl.when(me == 1)
    def _():
        for c in range(CHUNKS):
            rest = jnp.zeros((step, block), F32)
            for s in range(rows - 2):
                p1_copy(c, s).wait_recv()
                rest = rest + got1[s, chunk(c)].astype(F32)
            value = product(c_buf[chunk(c)] - rest, h1_buf[...], l1_buf[...])
            w_buf[chunk(c)] = value
            part0[chunk(c)] = product(value, h2_buf[...], l2_buf[...]).astype(SEND_TYPE)
            tt_copy(c).start()
            w_all[chunk(c), part(1)] = value.astype(BF16)
        for k in from_one:
            for c in range(CHUNKS):
                w_copy(c, k).start()

    lax.fori_loop(2, rows, kernel_block, 0)

    @pl.when(me == 0)
    def _():
        for c in range(CHUNKS):
            rest = jnp.zeros((step, block), F32)
            for s in range(rows - 2):
                p0_copy(c, s).wait_recv()
                rest = rest + got0[s, chunk(c)].astype(F32)
            tt_copy(c).wait_recv()
            rest = rest + got_t[chunk(c)].astype(F32)
            value = product(c_buf[chunk(c)] - rest, h1_buf[...], l1_buf[...])
            w_buf[chunk(c)] = value
            w_all[chunk(c), part(0)] = value.astype(BF16)
            for k in from_zero:
                w_copy(c, k).start()

    def w_wait(r):
        @pl.when(me != r)
        def _():
            for c in range(CHUNKS):
                remote(
                    w_all.at[chunk(c), part(r)],
                    w_all.at[chunk(c), part(r)],
                    w_send.at[c, 0],
                    w_recv.at[r, c],
                    0,
                ).wait_recv()

    def k_wait(r, carry):
        for j in range(tiles):
            k_copy(r, j, 1 - core).wait_recv()
        return carry

    def add_blocks(first, last, fresh):
        def add_tile(j, carry):
            at = pl.ds(pl.multiple_of(j * tile, 128), tile)
            value = jnp.dot(
                w_all[:, first * block : last * block],
                k_all[first * block : last * block, at],
                preferred_element_type=F32,
            )
            acc[:, at] = value if fresh else acc[:, at] + value
            return carry

        lax.fori_loop(0, 2 * tiles, add_tile, 0)

    def later_block(r, carry):
        @pl.when(r != me)
        def _():
            remote(
                w_all.at[:, part(r)], w_all.at[:, part(r)], c_send.at[0], c_recv.at[r], 0
            ).wait_recv()

        return k_wait(r, carry)

    lax.fori_loop(2, rows, later_block, 0)
    add_blocks(2, rows, True)
    w_wait(1)
    k_wait(1, 0)
    add_blocks(1, 2, False)
    k_wait(0, 0)
    w_wait(0)
    add_blocks(0, 1, False)

    def k_sent(r, carry):
        for j in range(tiles):
            k_copy(r, j, core).wait_send()
        return carry

    lax.fori_loop(0, rows, k_sent, 0)

    for k in range(1, rows):
        t_copy(k).wait_send()

    @pl.when(me >= 2)
    def _():
        for c in range(CHUNKS):
            p1_copy(c, me - 2).wait_send()
            p0_copy(c, me - 2).wait_send()
        for k in range(1, rows):
            c_copy(k).wait_send()

    @pl.when(me == 1)
    def _():
        for c in range(CHUNKS):
            tt_copy(c).wait_send()

    for r, peers in ((0, from_zero), (1, from_one)):

        @pl.when(me == r)
        def _():
            for c in range(CHUNKS):
                for k in peers:
                    w_copy(c, k).wait_send()


def on_device(
    coefficients, factor_panel, block_inverse, train_inputs, query_points, inv_length, amplitude
):
    rows = lax.axis_size("rows")
    m, block = coefficients.shape
    params = train_inputs.shape[0]
    width = query_points.shape[1] // (2 * rows)
    tile = 512 if width % 512 == 0 else width
    padded = -(-params // 16) * 16
    depth = -(-(6 * padded + 16) // 128) * 128
    anywhere = pl.BlockSpec(memory_space=pltpu.HBM)
    dma = pltpu.SemaphoreType.DMA
    vmem = pltpu.VMEM
    solved, summed = pl.pallas_call(
        functools.partial(kernel, rows),
        out_shape=(
            pltpu.VMEM((m, block), F32),
            pltpu.VMEM((m, 2 * width), F32),
        ),
        in_specs=[pl.BlockSpec(memory_space=pltpu.SMEM)] + [anywhere] * 5,
        out_specs=(pl.BlockSpec(memory_space=pltpu.VMEM),) * 2,
        scratch_shapes=[
            vmem((m, block), F32),
            vmem((block, block), F32),
            vmem((block, block), F32),
            vmem((block, block), F32),
            vmem((params, width), F32),
            vmem((rows, params, block), F32),
            vmem((block, block), BF16),
            vmem((block, block), BF16),
            vmem((block, block), BF16),
            vmem((block, block), BF16),
            vmem((m, block), SEND_TYPE),
            vmem((m, block), SEND_TYPE),
            vmem((rows - 2, m, block), SEND_TYPE),
            vmem((rows - 2, m, block), SEND_TYPE),
            vmem((m, block), SEND_TYPE),
            vmem((m, rows * block), BF16),
            vmem((block, depth), BF16),
            vmem((depth, width), BF16),
            vmem((rows * block, 2 * width), BF16),
            dma((6,)),
            dma((rows - 1,)),
            dma((rows,)),
            dma((CHUNKS,)),
            dma((rows - 2, CHUNKS)),
            dma((CHUNKS,)),
            dma((rows - 2, CHUNKS)),
            dma((CHUNKS,)),
            dma((CHUNKS,)),
            dma((rows - 1,)),
            dma((rows,)),
            dma((CHUNKS, rows - 1)),
            dma((2, CHUNKS)),
            dma((rows, width // tile)),
            dma((rows, width // tile)),
        ],
        compiler_params=pltpu.CompilerParams(
            collective_id=0, has_side_effects=True, vmem_limit_bytes=60 * 1024 * 1024
        ),
    )(inv_length, coefficients, factor_panel, block_inverse, train_inputs, query_points)
    weights = jnp.where(lax.axis_index("rows") < 2, solved, coefficients)
    return (weights, summed * amplitude[:, None])


def solution(mesh):
    return jax.shard_map(
        on_device,
        mesh=mesh,
        in_specs=(
            P("cols", "rows"),
            P("rows", None),
            P("rows", None),
            P(None, "rows"),
            P(),
            P(),
            P("cols"),
        ),
        out_specs=(P("cols", "rows"), P("cols", "rows")),
        check_vma=False,
    )
```
